128 devices in a mesh: band: 128 (over z, x, y, core).
Axes of the slice: x: 4, y: 4, z: 4, core: 2. Of those that a mesh axis runs over, the one named last changes fastest.
Arguments:
- features: bfloat16 [262144, 256], P('band'), may hold values from -6 to 6
- self_weight: bfloat16 [256, 256], replicated, may hold values from -0.375 to 0.375
- neighbor_weight: bfloat16 [256, 256], replicated, may hold values from -1.5 to 1.5
- bias_term: float32 [256], replicated, may hold values from -3 to 3
- tile_columns: int32 [2048, 6], P('band'), may hold values from 0 to 19, as said below
- tile_bits: int32 [2048, 6, 128, 128], P('band'), may hold values 0 or 1
- hub_slots: int32 [262144, 4], P('band'), may hold values from 0 to 4095
- hub_live: int32 [262144, 4], P('band'), may hold values 0 or 1
- degree: int32 [262144], P('band'), may hold values from 16 to 63
- hub_rows: int32 [4096], P('band'), may hold values from 0 to 2047
- cotangent: bfloat16 [262144, 256], P('band'), may hold values from -6 to 6
Outputs:
- hidden: bfloat16 [262144, 256], P('band')
- feature_grad: bfloat16 [262144, 256], P('band')
- self_grad: float32 [256, 256], replicated
- neighbor_grad: float32 [256, 256], replicated
- bias_grad: float32 [256], replicated
The draws below stay inside these ranges and needn't reach their ends.
Inputs may be any that keep to these rules, and one draw needn't show every extreme that they name: `tile_columns`: for row tile r of a band (r counted from 0 within the band), the listed column tiles lie in r to r + 4.
All inputs are finite; a program needn't handle non-finite values. No bound on the sum of `tile_bits` or of `hub_live` on one device may be relied on, other than what follows from the above.
Results may differ from the reference program's by a relative error of at most 0.007.
Values may be sent and summed in bfloat16 or wider, within the bound.
A program may use at most 128 MiB of HBM per device.

```python
import math
import jax
import jax.numpy as jnp
from jax import lax

F = 256
H = 256
TILE = 128
HT = 2
KT = 6
HK = 4
ROWS_DEV = 2048
HUB_DEV = 32
NODES = 262144
HUBS = 4096
N_BAND = 128


def draw_tile_columns(key, part):
    key = jax.random.fold_in(key, 11)
    tile_rows = ROWS_DEV // TILE
    offsets = jax.random.randint(key, (NODES // TILE, KT), 0, 2 * HT + 1)
    positions = jnp.arange(NODES // TILE, dtype=jnp.int32) % tile_rows
    return (offsets + positions[:, None]).astype(jnp.int32)


def touch_ends(entries, stream_key, low, largest):
    place = [jax.random.randint(jax.random.fold_in(stream_key, axis), (), 0, length) for axis, length in enumerate(entries.shape)]
    longest = entries.shape.index(max(entries.shape))
    beside = place[:longest] + [(place[longest] + 1) % entries.shape[longest]] + place[longest + 1:]
    return entries.at[tuple(place)].set(low).at[tuple(beside)].set(largest)


def shard_levels(key, dims, cuts, smallest, high):
    factor_of, own = 1.0, jax.random.fold_in(key, 6)
    for axis_at, shards_of in cuts:
        heights = jnp.exp(jax.random.uniform(jax.random.fold_in(own, axis_at), (shards_of,), jnp.float32, smallest / len(cuts), high / len(cuts)))
        factor_of = factor_of * jnp.repeat(heights, dims[axis_at] // shards_of).reshape([-1 if axis == axis_at else 1 for axis in range(len(dims))])
    return factor_of


def centred(rng, shape, deviation, limit, shards=(), kind=jnp.bfloat16):
    values = deviation * jax.random.normal(rng, shape, jnp.float32)
    if shards:
        values = values * shard_levels(rng, shape, shards, -0.22, 0.18)
    return jnp.clip(values, -limit, limit).astype(kind)


def setup_inputs(seed: int = 0) -> dict:
    arg_keys = jax.random.split(jax.random.key(seed), 12)
    return {
        "features": centred(arg_keys[0], (NODES, F), 1.0, 6.0, ((0, 128),)),
        "self_weight": centred(arg_keys[1], (F, H), F ** -0.5, 0.375),
        "neighbor_weight": centred(arg_keys[2], (F, H), (F // 16) ** -0.5, 1.5),
        "bias_term": centred(arg_keys[3], (H,), 0.5, 3.0, (), jnp.float32),
        "tile_columns": draw_tile_columns(jax.random.fold_in(arg_keys[11], 71), 0),
        "tile_bits": touch_ends((jax.random.randint(arg_keys[5], (NODES // TILE, KT, TILE, TILE), 0, 16) < 1).astype(jnp.int32), jax.random.fold_in(arg_keys[5], 1), 0, 1),
        "hub_slots": touch_ends(jax.random.randint(arg_keys[6], (NODES, HK), 0, HUBS), jax.random.fold_in(arg_keys[6], 1), 0, HUBS - 1).astype(jnp.int32),
        "hub_live": touch_ends((jax.random.randint(arg_keys[7], (NODES, HK), 0, 2) < 1).astype(jnp.int32), jax.random.fold_in(arg_keys[7], 1), 0, 1),
        "degree": touch_ends(jax.random.randint(arg_keys[8], (NODES,), 16, 64), jax.random.fold_in(arg_keys[8], 1), 16, 63).astype(jnp.int32),
        "hub_rows": touch_ends(jax.random.randint(arg_keys[9], (HUBS,), 0, ROWS_DEV), jax.random.fold_in(arg_keys[9], 1), 0, ROWS_DEV - 1).astype(jnp.int32),
        "cotangent": centred(arg_keys[10], (NODES, H), 1.0, 6.0, ((0, 128),)),
    }


def reference(features, self_weight, neighbor_weight, bias_term, tile_columns, tile_bits, hub_slots, hub_live, degree, hub_rows, cotangent):
    halo_rows = HT * TILE
    tile_rows = ROWS_DEV // TILE
    owners = jnp.arange(HUBS, dtype=jnp.int32) // HUB_DEV
    hub_node = owners * ROWS_DEV + hub_rows
    hub_table = features[hub_node]
    padded = jnp.pad(features, ((halo_rows, halo_rows), (0, 0)))
    columns = tile_columns.reshape(N_BAND, tile_rows, KT)
    blocks = tile_bits.reshape(N_BAND, tile_rows, KT, TILE, TILE)
    slots = hub_slots.reshape(N_BAND, ROWS_DEV, HK)
    lives = hub_live.reshape(N_BAND, ROWS_DEV, HK)

    def gather_band(items):
        band_index, column_set, block_set, slot_set, live_set = items
        extended = lax.dynamic_slice_in_dim(padded, band_index * ROWS_DEV, ROWS_DEV + 2 * halo_rows, 0)
        picked = extended.reshape(-1, TILE, F)[column_set].astype(jnp.float32)
        band_terms = jnp.einsum('rkab,rkbf->raf', block_set.astype(jnp.float32), picked).reshape(ROWS_DEV, F)
        hub_terms = jnp.einsum('rk,rkf->rf', live_set.astype(jnp.float32), hub_table[slot_set].astype(jnp.float32))
        return band_terms + hub_terms
    band_ids = jnp.arange(N_BAND, dtype=jnp.int32)
    sums = lax.map(gather_band, (band_ids, columns, blocks, slots, lives)).reshape(NODES, F)
    divisor = degree.astype(jnp.float32)[:, None]
    aggregate = (sums / divisor).astype(jnp.bfloat16)
    pre = jnp.dot(features, self_weight, preferred_element_type=jnp.float32)
    pre = pre + jnp.dot(aggregate, neighbor_weight, preferred_element_type=jnp.float32) + bias_term
    hidden = jax.nn.silu(pre).astype(jnp.bfloat16)
    sigma = jax.nn.sigmoid(pre)
    dpre = (cotangent.astype(jnp.float32) * sigma * (1.0 + pre * (1.0 - sigma))).astype(jnp.bfloat16)
    norm_scale = 1.0 / math.sqrt(NODES)
    self_grad = jnp.dot(features.T, dpre, preferred_element_type=jnp.float32) * norm_scale
    neighbor_grad = jnp.dot(aggregate.T, dpre, preferred_element_type=jnp.float32) * norm_scale
    bias_grad = lax.optimization_barrier(jnp.sum(dpre.astype(jnp.float32), axis=0)) * norm_scale
    dscaled = (jnp.dot(dpre, neighbor_weight.T, preferred_element_type=jnp.float32) / divisor).astype(jnp.bfloat16)
    dscaled_tiles = dscaled.reshape(N_BAND, tile_rows, TILE, F)

    def scatter_band(items):
        column_set, block_set, grad_set = items
        back = jnp.einsum('rkab,raf->rkbf', block_set.astype(jnp.float32), grad_set.astype(jnp.float32))
        placed = jax.ops.segment_sum(back.reshape(tile_rows * KT, TILE, F), column_set.reshape(-1), num_segments=tile_rows + 2 * HT)
        return placed.reshape(ROWS_DEV + 2 * halo_rows, F)
    ext_grad = lax.map(scatter_band, (columns, blocks, dscaled_tiles))
    middle = ext_grad[:, halo_rows:halo_rows + ROWS_DEV]
    low_rim = ext_grad[:, :halo_rows]
    high_rim = ext_grad[:, ROWS_DEV + halo_rows:]
    zero_rim = jnp.zeros((1, halo_rows, F), jnp.float32)
    from_next = jnp.concatenate([low_rim[1:], zero_rim], axis=0)
    from_prev = jnp.concatenate([zero_rim, high_rim[:-1]], axis=0)
    edge_grad = middle.at[:, :halo_rows].add(from_prev).at[:, ROWS_DEV - halo_rows:].add(from_next)
    dscaled_wide = dscaled.astype(jnp.float32)
    hub_total = jnp.zeros((HUBS, F), jnp.float32)
    for slot_index in range(HK):
        weighted = dscaled_wide * hub_live[:, slot_index].astype(jnp.float32)[:, None]
        hub_total = hub_total + jax.ops.segment_sum(weighted, hub_slots[:, slot_index], num_segments=HUBS)
    feature_grad = jnp.dot(dpre, self_weight.T, preferred_element_type=jnp.float32) + edge_grad.reshape(NODES, F)
    feature_grad = feature_grad.at[hub_node].add(hub_total).astype(jnp.bfloat16)
    return (hidden, feature_grad, self_grad, neighbor_grad, bias_grad)
```

```python
import math

import jax
import jax.numpy as jnp
from jax import lax
from jax.experimental import pallas as pl
from jax.experimental.pallas import tpu as pltpu
from jax.sharding import PartitionSpec as P

MESH = pl.DeviceIdType.MESH
BF = jnp.bfloat16
F32 = jnp.float32
I32 = jnp.int32
VMEM = pltpu.VMEM
DMA = pltpu.SemaphoreType.DMA

ROWS = 2048
WIDTH = 256
TILE = 128
TILES = 16
SLOTS = 6
HALO = 256
HUBS = 4096
ORDERS = ((0, 1, 2), (1, 2, 0))
TN = (((0,), (0,)), ((), ()))
NT = (((1,), (1,)), ((), ()))


def device(z, x, y, c):
    return ((z * 4 + x) * 4 + y) * 2 + c


def rows_at(start, size):
    return pl.ds(pl.multiple_of(start, size), size)


def remote(src, dst, send, recv, target):
    return pltpu.make_async_remote_copy(
        src_ref=src, dst_ref=dst, send_sem=send, recv_sem=recv, device_id=(target,), device_id_type=MESH
    )


def kernel(
    tcol, hrow, feat_hbm, bits_hbm, cot_hbm, ws, wn, bias, slots, live, deg,
    hidden_hbm, grad_hbm, sums,
    fext, bits, cot, hid, fgrad, table, counts, slotv, merged, band, pre0, rdeg,
    agg, dpre, dsc, hubf, base, rim_out, rim_in,
    hubp, hubc, hubs, hubz, accx, outx, hubx, accy, huby,
    gpart, gcore, gsum, gy, gsumx, gx, gz, gall,
    load_sem, bits_sem, store_sem, halo_s, halo_r, ag_s, ag_r, core_s, core_r, rim_s, rim_r,
    hc_s, hc_r, hz_s, hz_r, hx_s, hx_r, hy_s, hy_r,
    gc_s, gc_r, gy_s, gy_r, gx_s, gx_r, gz_s, gz_r, hgx_s, hgx_r, hgy_s, hgy_r, hgc_s, hgc_r,
):
    me = lax.axis_index("band")
    z, x, y, c = me // 32, (me // 8) % 4, (me // 2) % 4, me % 2
    at = (z, x, y)
    partner = device(z, x, y, 1 - c)
    after, before = (me + 1) % 128, (me + 127) % 128

    def peer(dim, k):
        place = list(at)
        place[dim] = (place[dim] + k) % 4
        return tuple(place)

    load_f = pltpu.make_async_copy(feat_hbm, fext.at[HALO : HALO + ROWS], load_sem.at[0])
    load_f.start()
    barrier = pltpu.get_barrier_semaphore()
    greeted = [partner, after, before]
    for k in (1, 2, 3):
        for dim in range(3):
            greeted.append(device(*peer(dim, k), c))
    for other in greeted:
        pl.semaphore_signal(barrier, inc=1, device_id=(other,), device_id_type=MESH)
    load_c = pltpu.make_async_copy(cot_hbm, cot, load_sem.at[1])
    bit_loads = []
    for r in range(TILES):
        load = pltpu.make_async_copy(bits_hbm.at[r], bits.at[r], bits_sem.at[r])
        load.start()
        bit_loads.append(load)
    load_c.start()

    lane = lax.broadcasted_iota(I32, (32, TILE), 1)
    sub = lax.broadcasted_iota(I32, (32, TILE), 0)
    hub_col = jnp.full((32, TILE), -1, I32)
    hub_row = jnp.full((1, TILE), -1, I32)
    lane1 = lax.broadcasted_iota(I32, (1, TILE), 1)
    for h in range(32):
        value = hrow[h]
        hub_col = jnp.where(sub == h, value, hub_col)
        hub_row = jnp.where((lane1 == h) | (lane1 == h + 32), value, hub_row)
    pick = jnp.concatenate(
        [(hub_col == lane + j * TILE).astype(F32).astype(BF) for j in range(TILES)], axis=1
    )
    load_f.wait()
    own = jnp.dot(pick, fext[HALO : HALO + ROWS, :], preferred_element_type=F32).astype(BF)
    table[0, z, x, y, c] = own[:, :TILE]
    table[1, z, x, y, c] = own[:, TILE:]

    pl.semaphore_wait(barrier, len(greeted))

    def line(half, place, core, free):
        index = [half] + [slice(None) if d in free else place[d] for d in range(3)] + [core]
        return table.at[tuple(index)]

    pending = []

    def gather_send(phase, half):
        dim, free = ORDERS[half][phase], ORDERS[half][:phase]
        block = line(half, at, c, free)
        for k in (1, 3, 2):
            copy = remote(block, block, ag_s.at[phase, half, k - 1], ag_r.at[phase, half, k - 1], device(*peer(dim, k), c))
            copy.start()
            pending.append(copy)

    def gather_recv(phase, half, k):
        dim, free = ORDERS[half][phase], ORDERS[half][:phase]
        block = line(half, peer(dim, 4 - k), c, free)
        remote(block, block, ag_s.at[phase, half, k - 1], ag_r.at[phase, half, k - 1], device(*peer(dim, k), c)).wait_recv()
        return block

    def gather_step(phase):
        for half in range(2):
            for k in (1, 3, 2):
                gather_recv(phase - 1, half, k)
            gather_send(phase, half)

    def core_send(block, n):
        copy = remote(block, block, core_s.at[n], core_r.at[n], partner)
        copy.start()
        pending.append(copy)

    def core_recv(half, place, n):
        block = line(half, place, 1 - c, ORDERS[half][:2])
        remote(block, block, core_s.at[n], core_r.at[n], partner).wait_recv()

    gather_send(0, 0)
    gather_send(0, 1)
    halo_low = remote(fext.at[HALO : 2 * HALO], fext.at[HALO + ROWS :], halo_s.at[0], halo_r.at[0], before)
    halo_high = remote(fext.at[ROWS : HALO + ROWS], fext.at[:HALO], halo_s.at[1], halo_r.at[1], after)
    halo_low.start()
    halo_high.start()
    pending.extend((halo_low, halo_high))

    slotv[...] = jnp.where(live[...] == 1, slots[...], -1)

    def build(first, last):
        span = 512

        def body(t, carry):
            block, col = first + t // 4, rows_at((t % 4) * span, span)
            ids = lax.broadcasted_iota(I32, (256, span), 0).astype(jnp.int16)
            total = jnp.zeros((256, span), BF)
            for k in range(4):
                value = jnp.broadcast_to(slotv[k : k + 1, col] - block * 256, (16, span)).astype(jnp.int16)
                value = jnp.broadcast_to(value[None], (16, 16, span)).reshape(256, span)
                total = total + jnp.where(value == ids, jnp.ones((), BF), jnp.zeros((), BF))
            counts[rows_at(block * 256, 256), col] = total
            return carry

        lax.fori_loop(0, (last - first) * 4, body, 0)

    build(0, 4)
    gather_step(1)
    build(4, 8)
    gather_step(2)
    build(8, 16)

    merged[0:4] = jnp.zeros((4, 5, TILE, TILE), BF)
    merged[20:24] = jnp.zeros((4, 5, TILE, TILE), BF)

    def merge(r, carry):
        pltpu.make_async_copy(bits_hbm.at[r], bits.at[r], bits_sem.at[r]).wait()
        weight = [[(tcol[k, r] == r + o).astype(F32) for k in range(SLOTS)] for o in range(5)]
        for s in range(4):
            part = pl.ds(s * 32, 32)
            total = [jnp.zeros((32, TILE), F32) for _ in range(5)]
            for k in range(SLOTS):
                value = bits[r, k, part, :].astype(F32)
                for o in range(5):
                    total[o] = total[o] + value * weight[o][k]
            for o in range(5):
                merged[r + 4, o, part, :] = total[o].astype(BF)
        row = 1.0 / deg[pl.ds(r, 1), :].astype(F32)
        rdeg[rows_at(r * TILE, TILE), :] = jnp.broadcast_to(row, (TILE, TILE)).T
        return carry

    lax.fori_loop(0, TILES, merge, 0)

    n = 0
    for half in range(2):
        core_send(line(half, at, c, ORDERS[half][:2]), n)
        n += 1
    for k in (1, 3, 2):
        for half in range(2):
            core_send(gather_recv(2, half, k), n)
            n += 1

    def forward(r, carry):
        left = jnp.concatenate([merged[r + 4, o] for o in range(5)], axis=1)
        right = fext[pl.ds(pl.multiple_of(r * TILE, TILE), 5 * TILE), :]
        here = rows_at(r * TILE, TILE)
        band[here, :] = jnp.dot(left, right, preferred_element_type=F32)
        return carry

    def own_term(j, carry):
        here = rows_at(j * 512, 512)
        value = jnp.dot(fext[rows_at(HALO + j * 512, 256), :], ws[...], preferred_element_type=F32)
        pre0[rows_at(j * 512, 256), :] = value + bias[...]
        value = jnp.dot(fext[rows_at(HALO + j * 512 + 256, 256), :], ws[...], preferred_element_type=F32)
        pre0[rows_at(j * 512 + 256, 256), :] = value + bias[...]
        return carry

    lax.fori_loop(0, 4, own_term, 0)
    lax.fori_loop(2, 14, forward, 0)
    halo_low.wait_recv()
    halo_high.wait_recv()
    fext[:HALO, :] = jnp.where(me == 0, 0.0, fext[:HALO, :].astype(F32)).astype(BF)
    fext[HALO + ROWS :, :] = jnp.where(me == 127, 0.0, fext[HALO + ROWS :, :].astype(F32)).astype(BF)
    lax.fori_loop(0, 2, forward, 0)
    lax.fori_loop(14, 16, forward, 0)

    n = 0
    for half in range(2):
        core_recv(half, at, n)
        n += 1
    for k in (1, 3, 2):
        for half in range(2):
            core_recv(half, peer(ORDERS[half][2], 4 - k), n)
            n += 1

    load_c.wait()

    def layer(j, carry):
        cols = rows_at(j * 512, 512)
        right = jnp.concatenate([table[0].reshape(HUBS, TILE), table[1].reshape(HUBS, TILE)], axis=1)
        hubf[...] = lax.dot_general(counts[:, cols], right, TN, preferred_element_type=F32)
        for half in range(2):
            here = rows_at(j * 512 + half * 256, 256)
            for s in range(4):
                part = rows_at(j * 512 + half * 256 + s * 64, 64)
                scale = rdeg[part, :]
                total = band[part, :] + hubf[half * 256 + s * 64 : half * 256 + s * 64 + 64, :]
                agg[part, :] = (total * jnp.concatenate([scale, scale], axis=1)).astype(BF)
            pre = pre0[here, :] + jnp.dot(agg[here, :], wn[...], preferred_element_type=F32)
            for s in range(4):
                part = rows_at(j * 512 + half * 256 + s * 64, 64)
                v = pre[s * 64 : s * 64 + 64, :]
                sig = 1.0 / (1.0 + jnp.exp(-v))
                act = v * sig
                hid[part, :] = act.astype(BF)
                dpre[part, :] = (cot[part, :].astype(F32) * sig * (1.0 + v - act)).astype(BF)
            back = lax.dot_general(dpre[here, :], wn[...], NT, preferred_element_type=F32)
            scale = rdeg[here, :]
            dsc[rows_at(512 + j * 512 + half * 256, 256), :] = (back * jnp.concatenate([scale, scale], axis=1)).astype(BF)
        return carry

    lax.fori_loop(0, 4, layer, 0)
    store_h = pltpu.make_async_copy(hid, hidden_hbm, store_sem.at[0])
    store_h.start()

    part = lax.dot_general(fext[HALO : HALO + ROWS, :], dpre[...], TN, preferred_element_type=F32)
    gpart[0, :, :, 0:16, :] = part.reshape(4, 4, 16, WIDTH)
    part = lax.dot_general(agg[...], dpre[...], TN, preferred_element_type=F32)
    gpart[1, :, :, 0:16, :] = part.reshape(4, 4, 16, WIDTH)
    gpart[:, :, :, 16:24, :] = jnp.zeros((2, 4, 4, 8, WIDTH), F32)
    part = jnp.dot(jnp.ones((16, ROWS), BF), dpre[...], preferred_element_type=F32)
    gpart[0, 0, 0, 16:24, :] = part[:8, :]
    copy_gc = remote(gpart.at[1 - c], gcore, gc_s.at[0], gc_r.at[0], partner)
    copy_gc.start()
    pending.append(copy_gc)

    def g_core():
        copy_gc.wait_recv()
        gsum[...] = gpart[c] + gcore[...]
        for k in (1, 3, 2):
            copy = remote(gsum.at[(y + k) % 4], gy.at[k - 1], gy_s.at[k - 1], gy_r.at[k - 1], device(*peer(2, k), c))
            copy.start()
            pending.append(copy)

    def g_y():
        for k in (1, 2, 3):
            remote(gsum.at[y], gy.at[k - 1], gy_s.at[k - 1], gy_r.at[k - 1], me).wait_recv()
        gsumx[...] = gsum[y] + gy[0] + gy[1] + gy[2]
        for k in (1, 3, 2):
            copy = remote(gsumx.at[(x + k) % 4], gx.at[k - 1], gx_s.at[k - 1], gx_r.at[k - 1], device(*peer(1, k), c))
            copy.start()
            pending.append(copy)

    def g_x():
        for k in (1, 2, 3):
            remote(gsumx.at[x], gx.at[k - 1], gx_s.at[k - 1], gx_r.at[k - 1], me).wait_recv()
        gz[z] = gsumx[x] + gx[0] + gx[1] + gx[2]
        for k in (1, 3, 2):
            copy = remote(gz.at[z], gz.at[z], gz_s.at[k - 1], gz_r.at[k - 1], device(*peer(0, k), c))
            copy.start()
            pending.append(copy)

    def g_z():
        for k in (1, 2, 3):
            slot = gz.at[(z + 4 - k) % 4]
            remote(slot, slot, gz_s.at[k - 1], gz_r.at[k - 1], me).wait_recv()
        gall[c, y, x] = (gz[0] + gz[1] + gz[2] + gz[3]) * (1.0 / 512.0)
        piece = gall.at[c, y, x]
        for k in (1, 3, 2):
            copy = remote(piece, piece, hgx_s.at[k - 1], hgx_r.at[k - 1], device(*peer(1, k), c))
            copy.start()
            pending.append(copy)

    def g_gather_x():
        for k in (1, 2, 3):
            slot = gall.at[c, y, (x + 4 - k) % 4]
            remote(slot, slot, hgx_s.at[k - 1], hgx_r.at[k - 1], me).wait_recv()
        piece = gall.at[c, y]
        for k in (1, 3, 2):
            copy = remote(piece, piece, hgy_s.at[k - 1], hgy_r.at[k - 1], device(*peer(2, k), c))
            copy.start()
            pending.append(copy)

    def g_gather_y():
        for k in (1, 2, 3):
            slot = gall.at[c, (y + 4 - k) % 4]
            remote(slot, slot, hgy_s.at[k - 1], hgy_r.at[k - 1], me).wait_recv()
        piece = gall.at[c]
        copy = remote(piece, piece, hgc_s.at[0], hgc_r.at[0], partner)
        copy.start()
        pending.append(copy)

    def g_gather_core():
        slot = gall.at[1 - c]
        remote(slot, slot, hgc_s.at[0], hgc_r.at[0], partner).wait_recv()
        for w in range(2):
            sums[w * 256 : (w + 1) * 256, :] = gall[w, :, :, 0:16, :].reshape(256, WIDTH)
        sums[512:520, :] = gall[0, 0, 0, 16:24, :]

    def hub_part(zc):
        def body(j, carry):
            left = counts[rows_at(zc * 1024 + j * 512, 512), :]
            value = jnp.dot(left, dsc[512 : 512 + ROWS, :], preferred_element_type=F32)
            hubp[zc, pl.ds(j * 2, 2)] = value.astype(BF).reshape(2, 4, 2, 32, WIDTH)
            return carry

        lax.fori_loop(0, 2, body, 0)
        copy = remote(hubp.at[zc, :, :, 1 - c], hubc.at[zc], hc_s.at[zc], hc_r.at[zc], partner)
        copy.start()
        pending.append(copy)

    def hub_core_recv(zc):
        remote(hubp.at[zc, :, :, 1 - c], hubc.at[zc], hc_s.at[zc], hc_r.at[zc], partner).wait_recv()

    def hub_z_send(k):
        zc = (z + k) % 4
        hub_core_recv(zc)
        hubs[k - 1] = (hubp[zc, :, :, c].astype(F32) + hubc[zc].astype(F32)).astype(BF)
        copy = remote(hubs.at[k - 1], hubz.at[k - 1], hz_s.at[k - 1], hz_r.at[k - 1], device(*peer(0, k), c))
        copy.start()
        pending.append(copy)

    def hub_x_send():
        hub_core_recv(z)
        for k in (1, 2, 3):
            remote(hubs.at[k - 1], hubz.at[k - 1], hz_s.at[k - 1], hz_r.at[k - 1], me).wait_recv()
        for i in range(4):
            total = hubp[z, i, :, c].astype(F32) + hubc[z, i].astype(F32)
            for k in range(3):
                total = total + hubz[k, i].astype(F32)
            accx[i] = total
            outx[i] = total.astype(BF)
        for k in (1, 3, 2):
            copy = remote(outx.at[(x + k) % 4], hubx.at[k - 1], hx_s.at[k - 1], hx_r.at[k - 1], device(*peer(1, k), c))
            copy.start()
            pending.append(copy)

    def hub_y_send():
        for k in (1, 2, 3):
            remote(outx.at[x], hubx.at[k - 1], hx_s.at[k - 1], hx_r.at[k - 1], me).wait_recv()
        total = accx[x]
        for k in range(3):
            total = total + hubx[k].astype(F32)
        accy[...] = total
        for k in (1, 3, 2):
            copy = remote(accy.at[(y + k) % 4], huby.at[k - 1], hy_s.at[k - 1], hy_r.at[k - 1], device(*peer(2, k), c))
            copy.start()
            pending.append(copy)

    def hub_total():
        for k in (1, 2, 3):
            remote(accy.at[y], huby.at[k - 1], hy_s.at[k - 1], hy_r.at[k - 1], me).wait_recv()
        return accy[y] + huby[0] + huby[1] + huby[2]

    hub_part((z + 2) % 4)
    hub_part((z + 1) % 4)
    hub_z_send(2)
    g_core()
    hub_part((z + 3) % 4)
    hub_z_send(1)
    hub_part(z)
    hub_z_send(3)
    g_y()

    dsc[0:512, :] = jnp.zeros((512, WIDTH), BF)
    dsc[512 + ROWS :, :] = jnp.zeros((512, WIDTH), BF)

    def transposed(t):
        left = jnp.concatenate([merged[t + q, 4 - q] for q in range(5)], axis=0)
        right = dsc[pl.ds(pl.multiple_of(t * TILE, TILE), 5 * TILE), :]
        return lax.dot_general(left, right, TN, preferred_element_type=F32)

    for side, start in ((0, 0), (1, 18)):
        for i in range(2):
            rim_out[side, i * TILE : (i + 1) * TILE, :] = transposed(start + i).astype(BF)
    rim_low = remote(rim_out.at[0], rim_in.at[0], rim_s.at[0], rim_r.at[0], before)
    rim_high = remote(rim_out.at[1], rim_in.at[1], rim_s.at[1], rim_r.at[1], after)
    rim_low.start()
    rim_high.start()
    pending.extend((rim_low, rim_high))

    def interior(t, carry):
        here = rows_at(t * TILE, TILE)
        value = transposed(t + 2)
        value = value + lax.dot_general(dpre[here, :], ws[...], NT, preferred_element_type=F32)
        base[here, :] = value
        return carry

    lax.fori_loop(0, 8, interior, 0)
    g_x()
    lax.fori_loop(8, 16, interior, 0)
    hub_x_send()
    g_z()
    rim_low.wait_recv()
    rim_high.wait_recv()
    low = jnp.where(me == 0, 0.0, rim_in[1].astype(F32))
    base[:HALO, :] = base[:HALO, :] + low
    high = jnp.where(me == 127, 0.0, rim_in[0].astype(F32))
    base[ROWS - HALO :, :] = base[ROWS - HALO :, :] + high
    hub_y_send()
    g_gather_x()
    total = hub_total()
    g_gather_y()
    upper = total.astype(BF)
    lower = (total - upper.astype(F32)).astype(BF)
    right = jnp.concatenate([upper, lower, jnp.zeros((64, WIDTH), BF)], axis=0)

    def finish(j, carry):
        here = rows_at(j * 256, 256)
        ids = lax.broadcasted_iota(I32, (256, TILE), 0) + j * 256
        place = (ids == hub_row).astype(F32).astype(BF)
        value = base[here, :] + jnp.dot(place, right, preferred_element_type=F32)
        fgrad[here, :] = value.astype(BF)
        return carry

    lax.fori_loop(0, 8, finish, 0)
    store_g = pltpu.make_async_copy(fgrad, grad_hbm, store_sem.at[1])
    store_g.start()
    g_gather_core()
    for copy in pending:
        copy.wait_send()
    store_h.wait()
    store_g.wait()


SCRATCH = [
    VMEM((ROWS + 2 * HALO, WIDTH), BF),
    VMEM((TILES, SLOTS, TILE, TILE), I32),
    VMEM((ROWS, WIDTH), BF),
    VMEM((ROWS, WIDTH), BF),
    VMEM((ROWS, WIDTH), BF),
    VMEM((2, 4, 4, 4, 2, 32, TILE), BF),
    VMEM((HUBS, ROWS), BF),
    VMEM((4, ROWS), I32),
    VMEM((24, 5, TILE, TILE), BF),
    VMEM((ROWS, WIDTH), F32),
    VMEM((ROWS, WIDTH), F32),
    VMEM((ROWS, TILE), F32),
    VMEM((ROWS, WIDTH), BF),
    VMEM((ROWS, WIDTH), BF),
    VMEM((ROWS + 1024, WIDTH), BF),
    VMEM((512, WIDTH), F32),
    VMEM((ROWS, WIDTH), F32),
    VMEM((2, HALO, WIDTH), BF),
    VMEM((2, HALO, WIDTH), BF),
    VMEM((4, 4, 4, 2, 32, WIDTH), BF),
    VMEM((4, 4, 4, 32, WIDTH), BF),
    VMEM((3, 4, 4, 32, WIDTH), BF),
    VMEM((3, 4, 4, 32, WIDTH), BF),
    VMEM((4, 4, 32, WIDTH), F32),
    VMEM((4, 4, 32, WIDTH), BF),
    VMEM((3, 4, 32, WIDTH), BF),
    VMEM((4, 32, WIDTH), F32),
    VMEM((3, 32, WIDTH), F32),
    VMEM((2, 4, 4, 24, WIDTH), F32),
    VMEM((4, 4, 24, WIDTH), F32),
    VMEM((4, 4, 24, WIDTH), F32),
    VMEM((3, 4, 24, WIDTH), F32),
    VMEM((4, 24, WIDTH), F32),
    VMEM((3, 24, WIDTH), F32),
    VMEM((4, 24, WIDTH), F32),
    VMEM((2, 4, 4, 24, WIDTH), F32),
    DMA((2,)), DMA((TILES,)), DMA((2,)),
    DMA((2,)), DMA((2,)),
    DMA((3, 2, 3)), DMA((3, 2, 3)),
    DMA((8,)), DMA((8,)),
    DMA((2,)), DMA((2,)),
    DMA((4,)), DMA((4,)),
    DMA((3,)), DMA((3,)), DMA((3,)), DMA((3,)), DMA((3,)), DMA((3,)),
    DMA((1,)), DMA((1,)),
    DMA((3,)), DMA((3,)), DMA((3,)), DMA((3,)), DMA((3,)), DMA((3,)),
    DMA((3,)), DMA((3,)), DMA((3,)), DMA((3,)),
    DMA((1,)), DMA((1,)),
]


def local(
    features, self_weight, neighbor_weight, bias_term, tile_columns, tile_bits,
    hub_slots, hub_live, degree, hub_rows, cotangent,
):
    smem = pl.BlockSpec(memory_space=pltpu.SMEM)
    vmem = pl.BlockSpec(memory_space=VMEM)
    hbm = pl.BlockSpec(memory_space=pl.ANY)
    hidden, feature_grad, sums = pl.pallas_call(
        kernel,
        out_shape=(
            jax.ShapeDtypeStruct((ROWS, WIDTH), BF),
            jax.ShapeDtypeStruct((ROWS, WIDTH), BF),
            jax.ShapeDtypeStruct((520, WIDTH), F32),
        ),
        in_specs=[smem, smem, hbm, hbm, hbm] + [vmem] * 6,
        out_specs=(hbm, hbm, vmem),
        scratch_shapes=SCRATCH,
        name="sage_layer",
        compiler_params=pltpu.CompilerParams(
            collective_id=0, has_side_effects=True, vmem_limit_bytes=60 * 2**20
        ),
    )(
        tile_columns.T, hub_rows, features, tile_bits, cotangent, self_weight, neighbor_weight,
        bias_term.reshape(1, WIDTH), hub_slots.T, hub_live.T, degree.reshape(TILES, TILE),
    )
    return hidden, feature_grad, sums[:256], sums[256:512], sums[512]


def solution(mesh):
    placed = (
        P("band", None), P(), P(), P(), P("band", None), P("band", None, None, None),
        P("band", None), P("band", None), P("band"), P("band"), P("band", None),
    )
    return jax.shard_map(
        local,
        mesh=mesh,
        in_specs=placed,
        out_specs=(P("band", None), P("band", None), P(), P(), P()),
        check_vma=False,
    )
```

```python
import math

import jax
import jax.numpy as jnp
from jax import lax
from jax.experimental import pallas as pl
from jax.experimental.pallas import tpu as pltpu
from jax.sharding import PartitionSpec as P

MESH = pl.DeviceIdType.MESH
BF = jnp.bfloat16
F32 = jnp.float32
I32 = jnp.int32
VMEM = pltpu.VMEM
DMA = pltpu.SemaphoreType.DMA

ROWS = 2048
WIDTH = 256
TILE = 128
TILES = 16
SLOTS = 6
HALO = 256
HUBS = 4096
ORDERS = ((0, 1, 2), (1, 2, 0))
PLANE = [(i, j) for i in range(4) for j in range(4) if (i, j) != (0, 0)]
PLANE.sort(key=lambda step: -min(step[0], 4 - step[0]) - min(step[1], 4 - step[1]))
TN = (((0,), (0,)), ((), ()))
NT = (((1,), (1,)), ((), ()))


def device(z, x, y, c):
    return ((z * 4 + x) * 4 + y) * 2 + c


def rows_at(start, size):
    return pl.ds(pl.multiple_of(start, size), size)


def remote(src, dst, send, recv, target):
    return pltpu.make_async_remote_copy(
        src_ref=src, dst_ref=dst, send_sem=send, recv_sem=recv, device_id=(target,), device_id_type=MESH
    )


def kernel(
    tcol, hrow, feat_hbm, bits_hbm, cot_hbm, ws_hbm, wn_hbm, bias_hbm, slots_hbm, live_hbm, deg_hbm,
    hid, fgrad, sums,
    feat, low, high, bits, cot, ws, wn, bias, slots, live, deg, table, counts, slot_low, slot_high, onehot, merged, band, pre0,
    rdeg, agg, dpre, dsc, base, rim_out, rim_in,
    hubp, hubc, hubs, recv_a, sum_a, out_b, recv_b, sum_b, recv_c,
    gpart, gcore, gsum, gxy, gz, gall,
    load_sem, bits_sem, halo_s, halo_r, ag_s, ag_r, line_s, line_r, core_s, core_r, rim_s, rim_r,
    hc_s, hc_r, ha_s, ha_r, hb_s, hb_r, hd_s, hd_r,
    gc_s, gc_r, gxy_s, gxy_r, gz_s, gz_r, gg_s, gg_r, gh_s, gh_r,
):
    me = lax.axis_index("band")
    z, x, y, c = me // 32, (me // 8) % 4, (me // 2) % 4, me % 2
    at = (z, x, y)
    partner = device(z, x, y, 1 - c)
    after, before = (me + 1) % 128, (me + 127) % 128

    def peer(dim, k):
        place = list(at)
        place[dim] = (place[dim] + k) % 4
        return tuple(place)

    load_f = pltpu.make_async_copy(feat_hbm, feat, load_sem.at[0])
    load_f.start()
    small = [
        pltpu.make_async_copy(source, target, load_sem.at[2 + i])
        for i, (source, target) in enumerate(
            ((slots_hbm, slots), (live_hbm, live), (ws_hbm, ws), (wn_hbm, wn), (bias_hbm, bias), (deg_hbm, deg))
        )
    ]
    barrier = pltpu.get_barrier_semaphore()
    greeted = [partner, after, before]
    greeted.extend(device(*peer(0, k), c) for k in (1, 2, 3))
    greeted.extend(device(z, (x + i) % 4, (y + j) % 4, c) for i, j in PLANE)
    for other in greeted:
        pl.semaphore_signal(barrier, inc=1, device_id=(other,), device_id_type=MESH)
    for load in small:
        load.start()
    load_c = pltpu.make_async_copy(cot_hbm, cot, load_sem.at[1])
    bit_loads = []
    for r in range(TILES):
        load = pltpu.make_async_copy(bits_hbm.at[r], bits.at[r], bits_sem.at[r])
        load.start()
        bit_loads.append(load)
    load_c.start()

    lane = lax.broadcasted_iota(I32, (32, TILE), 1)
    sub = lax.broadcasted_iota(I32, (32, TILE), 0)
    hub_col = jnp.full((32, TILE), -1, I32)
    hub_row = jnp.full((1, TILE), -1, I32)
    lane1 = lax.broadcasted_iota(I32, (1, TILE), 1)
    for h in range(32):
        value = hrow[h]
        hub_col = jnp.where(sub == h, value, hub_col)
        hub_row = jnp.where((lane1 == h) | (lane1 == h + 32), value, hub_row)
    pick = jnp.concatenate(
        [(hub_col == lane + j * TILE).astype(F32).astype(BF) for j in range(TILES)], axis=1
    )
    load_f.wait()
    own = jnp.dot(pick, feat[...].reshape(ROWS, WIDTH), preferred_element_type=F32).astype(BF)
    table[0, z, x, y, c] = own[:, :TILE]
    table[1, z, x, y, c] = own[:, TILE:]

    pl.semaphore_wait(barrier, len(greeted))

    def line(half, place, core, free):
        index = [half] + [slice(None) if d in free else place[d] for d in range(3)] + [core]
        return table.at[tuple(index)]

    pending = []

    def gather_send(phase, half):
        dim, free = ORDERS[half][phase], ORDERS[half][:phase]
        block = line(half, at, c, free)
        for k in (1, 3, 2):
            copy = remote(block, block, ag_s.at[phase, half, k - 1], ag_r.at[phase, half, k - 1], device(*peer(dim, k), c))
            copy.start()
            pending.append(copy)

    def gather_recv(phase, half, k):
        dim, free = ORDERS[half][phase], ORDERS[half][:phase]
        block = line(half, peer(dim, 4 - k), c, free)
        remote(block, block, ag_s.at[phase, half, k - 1], ag_r.at[phase, half, k - 1], device(*peer(dim, k), c)).wait_recv()

    def line_send(half, k):
        middle, last = ORDERS[half][1:]
        block = line(half, peer(middle, (4 - k) % 4), c, ORDERS[half][:1])
        for i in (1, 3, 2):
            copy = remote(block, block, line_s.at[half, k, i - 1], line_r.at[half, k, i - 1], device(*peer(last, i), c))
            copy.start()
            pending.append(copy)

    def line_recv(half, i):
        middle, last = ORDERS[half][1:]
        place = list(peer(last, 4 - i))
        for k in range(4):
            piece = list(place)
            piece[middle] = (piece[middle] + 4 - k) % 4
            block = line(half, piece, c, ORDERS[half][:1])
            remote(block, block, line_s.at[half, k, i - 1], line_r.at[half, k, i - 1], partner).wait_recv()
        return line(half, place, c, ORDERS[half][:2])

    def core_send(block, n):
        copy = remote(block, block, core_s.at[n], core_r.at[n], partner)
        copy.start()
        pending.append(copy)

    def core_recv(half, place, n):
        block = line(half, place, 1 - c, ORDERS[half][:2])
        remote(block, block, core_s.at[n], core_r.at[n], partner).wait_recv()

    gather_send(0, 0)
    gather_send(0, 1)

    for load in small:
        load.wait()
    named = jnp.where(live[...] == 1, slots[...], -1)
    slot_low[...] = named & 255
    slot_high[...] = named >> 8
    span = 512

    def build(j, carry):
        cols = rows_at(j * span, span)
        ids = lax.broadcasted_iota(I32, (256, span), 0).astype(jnp.int16)
        for k in range(4):
            value = jnp.broadcast_to(slot_low[k : k + 1, cols], (16, span)).astype(jnp.int16)
            value = jnp.broadcast_to(value[None], (16, 16, span)).reshape(256, span)
            onehot[k] = jnp.where(value == ids, jnp.ones((), BF), jnp.zeros((), BF))

        def block(h, carry):
            total = jnp.zeros((256, span), BF)
            for k in range(4):
                keep = jnp.broadcast_to(jnp.where(slot_high[k : k + 1, cols] == h, 1.0, 0.0), (16, span)).astype(BF)
                keep = jnp.broadcast_to(keep[None], (16, 16, span)).reshape(256, span)
                total = total + onehot[k] * keep
            counts[rows_at(h * 256, 256), cols] = total
            return carry

        return lax.fori_loop(0, HUBS // 256, block, carry)

    lax.fori_loop(0, 2, build, 0)
    for half in range(2):
        for k in (1, 3, 2):
            gather_recv(0, half, k)
        gather_send(1, half)
        line_send(half, 0)
    lax.fori_loop(2, 4, build, 0)
    for k in (1, 3, 2):
        for half in range(2):
            gather_recv(1, half, k)
            line_send(half, k)
    halo_low = remote(feat.at[0:2], high.at[4:6], halo_s.at[0], halo_r.at[0], before)
    halo_high = remote(feat.at[14:16], low.at[0:2], halo_s.at[1], halo_r.at[1], after)
    halo_low.start()
    halo_high.start()
    pending.extend((halo_low, halo_high))
    for half in range(2):
        core_send(line(half, at, c, ORDERS[half][:2]), half)

    def own_term(j, carry):
        here = rows_at(j * 256, 256)
        pre0[here, :] = jnp.dot(feat[pl.ds(j * 2, 2)].reshape(256, WIDTH), ws[...], preferred_element_type=F32) + bias[...]
        return carry

    def divide(r, carry):
        row = 1.0 / deg[pl.ds(r, 1), :].astype(F32)
        rdeg[rows_at(r * TILE, TILE), :] = jnp.broadcast_to(row, (TILE, TILE)).T
        return carry

    def forward(rows, first):
        def body(r, carry):
            pltpu.make_async_copy(bits_hbm.at[r], bits.at[r], bits_sem.at[r]).wait()
            left = jnp.concatenate([bits[r, k].astype(F32).astype(BF) for k in range(SLOTS)], axis=1)
            right = jnp.concatenate([rows[jnp.clip(tcol[k, r] - first, 0, rows.shape[0] - 1)] for k in range(SLOTS)], axis=0)
            band[rows_at(r * TILE, TILE), :] = jnp.dot(left, right, preferred_element_type=F32)
            return carry

        return body

    lax.fori_loop(0, 8, own_term, 0)
    lax.fori_loop(0, TILES, divide, 0)
    lax.fori_loop(2, 8, forward(feat, 2), 0)
    n = 2
    for k in (1, 3):
        for half in range(2):
            core_send(line_recv(half, k), n)
            n += 1
    lax.fori_loop(8, 14, forward(feat, 2), 0)
    for half in range(2):
        core_send(line_recv(half, 2), n)
        n += 1
    low[2:6] = feat[0:4]
    high[0:4] = feat[12:16]
    halo_low.wait_recv()
    halo_high.wait_recv()
    low[0:2] = jnp.where(me == 0, 0.0, low[0:2].astype(F32)).astype(BF)
    high[4:6] = jnp.where(me == 127, 0.0, high[4:6].astype(F32)).astype(BF)
    lax.fori_loop(0, 2, forward(low, 0), 0)
    lax.fori_loop(14, 16, forward(high, 14), 0)

    n = 0
    for k in (0, 1, 3, 2):
        for half in range(2):
            core_recv(half, peer(ORDERS[half][2], (4 - k) % 4), n)
            n += 1

    load_c.wait()

    def layer(j, carry):
        cols = rows_at(j * 1024, 1024)
        right = jnp.concatenate([table[0].reshape(HUBS, TILE), table[1].reshape(HUBS, TILE)], axis=1)
        base[cols, :] = lax.dot_general(counts[:, cols], right, TN, preferred_element_type=F32)

        def chunk(i, carry):
            start = j * 1024 + i * 256
            here = rows_at(start, 256)
            for s in range(4):
                part = rows_at(start + s * 64, 64)
                scale = rdeg[part, :]
                total = band[part, :] + base[part, :]
                agg[part, :] = (total * jnp.concatenate([scale, scale], axis=1)).astype(BF)
            pre = pre0[here, :] + jnp.dot(agg[here, :], wn[...], preferred_element_type=F32)
            for s in range(4):
                part = rows_at(start + s * 64, 64)
                v = pre[s * 64 : s * 64 + 64, :]
                sig = 1.0 / (1.0 + jnp.exp(-v))
                act = v * sig
                hid[part, :] = act.astype(BF)
                dpre[part, :] = (cot[part, :].astype(F32) * sig * (1.0 + v - act)).astype(BF)
            back = lax.dot_general(dpre[here, :], wn[...], NT, preferred_element_type=F32)
            scale = rdeg[here, :]
            dsc[rows_at(512 + start, 256), :] = (back * jnp.concatenate([scale, scale], axis=1)).astype(BF)
            return carry

        return lax.fori_loop(0, 4, chunk, carry)

    lax.fori_loop(0, 2, layer, 0)

    gpart[:, :, :, 32:40, :] = jnp.zeros((2, 4, 4, 8, TILE), F32)
    for which, left in ((0, feat[...].reshape(ROWS, WIDTH)), (1, agg[...])):
        part = lax.dot_general(left, dpre[...], TN, preferred_element_type=F32).reshape(4, 4, 16, WIDTH)
        gpart[which, :, :, 0:16, :] = part[..., :TILE]
        gpart[which, :, :, 16:32, :] = part[..., TILE:]
    part = jnp.dot(jnp.ones((16, ROWS), BF), dpre[...], preferred_element_type=F32)
    row8 = lax.broadcasted_iota(I32, (8, TILE), 0)
    gpart[0, 0, 0, 32:40, :] = jnp.where(row8 == 0, part[:8, :TILE], jnp.where(row8 == 1, part[:8, TILE:], 0.0))
    copy_gc = remote(gpart.at[1 - c], gcore, gc_s.at[0], gc_r.at[0], partner)
    copy_gc.start()
    pending.append(copy_gc)

    def g_core():
        copy_gc.wait_recv()
        gsum[...] = gpart[c] + gcore[...]
        for n, (i, j) in enumerate(PLANE):
            there = ((x + i) % 4, (y + j) % 4)
            copy = remote(gsum.at[there[1], there[0]], gxy.at[n], gxy_s.at[n], gxy_r.at[n], device(z, *there, c))
            copy.start()
            pending.append(copy)

    def g_plane():
        total = gsum[y, x]
        for n in range(15):
            remote(gsum.at[y, x], gxy.at[n], gxy_s.at[n], gxy_r.at[n], partner).wait_recv()
            total = total + gxy[n]
        gz[z] = total
        for k in (1, 3, 2):
            copy = remote(gz.at[z], gz.at[z], gz_s.at[k - 1], gz_r.at[k - 1], device(*peer(0, k), c))
            copy.start()
            pending.append(copy)

    def g_z():
        for k in (1, 2, 3):
            slot = gz.at[(z + 4 - k) % 4]
            remote(slot, slot, gz_s.at[k - 1], gz_r.at[k - 1], partner).wait_recv()
        gall[c, y, x] = (gz[0] + gz[1] + gz[2] + gz[3]) * (1.0 / 512.0)
        piece = gall.at[c, y, x]
        for n, (i, j) in enumerate(PLANE):
            copy = remote(piece, piece, gg_s.at[n], gg_r.at[n], device(z, (x + i) % 4, (y + j) % 4, c))
            copy.start()
            pending.append(copy)

    def g_gather():
        for n, (i, j) in enumerate(PLANE):
            slot = gall.at[c, (y + 4 - j) % 4, (x + 4 - i) % 4]
            remote(slot, slot, gg_s.at[n], gg_r.at[n], partner).wait_recv()
        piece = gall.at[c]
        copy = remote(piece, piece, gh_s.at[0], gh_r.at[0], partner)
        copy.start()
        pending.append(copy)

    def g_done():
        slot = gall.at[1 - c]
        remote(slot, slot, gh_s.at[0], gh_r.at[0], partner).wait_recv()

    def hub_part(zc):
        left = counts[rows_at(zc * 1024, 1024), :]
        value = jnp.dot(left, dsc[512 : 512 + ROWS, :], preferred_element_type=F32)
        hubp[zc] = value.astype(BF).reshape(4, 4, 2, 32, WIDTH)
        copy = remote(hubp.at[zc, :, :, 1 - c], hubc.at[zc], hc_s.at[zc], hc_r.at[zc], partner)
        copy.start()
        pending.append(copy)

    def hub_add(zc):
        remote(hubp.at[zc, :, :, 1 - c], hubc.at[zc], hc_s.at[zc], hc_r.at[zc], partner).wait_recv()
        for i in range(4):
            total = (hubp[zc, i, :, c].astype(F32) + hubc[zc, i].astype(F32)).astype(BF)
            hubs[0, zc, i] = total[..., :TILE]
            hubs[1, zc, i] = total[..., TILE:]

    def send_a(zc):
        for k in (2, 1, 3):
            for half in range(2):
                source = hubs.at[0, zc, (x + k) % 4] if half == 0 else hubs.at[1, zc, :, (y + k) % 4]
                copy = remote(
                    source, recv_a.at[half, k - 1, zc], ha_s.at[half, k - 1, zc], ha_r.at[half, k - 1, zc],
                    device(*peer(1 + half, k), c),
                )
                copy.start()
                pending.append(copy)

    def collect(zc):
        for k in range(3):
            for half in range(2):
                block = recv_a.at[half, k, zc]
                remote(block, block, ha_s.at[half, k, zc], ha_r.at[half, k, zc], partner).wait_recv()
        totals = []
        for half in range(2):
            total = (hubs[0, zc, x] if half == 0 else hubs[1, zc, :, y]).astype(F32)
            for k in range(3):
                total = total + recv_a[half, k, zc].astype(F32)
            totals.append(total)
        return totals

    def send_b(k):
        for half, total in enumerate(collect((z + k) % 4)):
            out_b[k - 1, half] = total.astype(BF)
        copy = remote(out_b.at[k - 1], recv_b.at[k - 1], hb_s.at[k - 1], hb_r.at[k - 1], device(*peer(0, k), c))
        copy.start()
        pending.append(copy)

    def send_c():
        for k in range(3):
            remote(recv_b.at[k], recv_b.at[k], hb_s.at[k], hb_r.at[k], partner).wait_recv()
        for half in range(2):
            total = sum_a[half]
            for k in range(3):
                total = total + recv_b[k, half].astype(F32)
            sum_b[half] = total
        for k in (2, 1, 3):
            for half, dim in ((0, 2), (1, 1)):
                copy = remote(
                    sum_b.at[half, (at[dim] + k) % 4], recv_c.at[half, k - 1],
                    hd_s.at[half, k - 1], hd_r.at[half, k - 1], device(*peer(dim, k), c),
                )
                copy.start()
                pending.append(copy)

    def hub_total(half):
        for k in range(3):
            remote(recv_c.at[half, k], recv_c.at[half, k], hd_s.at[half, k], hd_r.at[half, k], partner).wait_recv()
        return sum_b[half, at[2 - half]] + recv_c[half, 0] + recv_c[half, 1] + recv_c[half, 2]

    def merge(r, carry):
        weight = [[(tcol[k, r] == r + o).astype(F32) for k in range(SLOTS)] for o in range(5)]
        for s in range(4):
            part = pl.ds(s * 32, 32)
            total = [jnp.zeros((32, TILE), F32) for _ in range(5)]
            for k in range(SLOTS):
                value = bits[r, k, part, :].astype(F32)
                for o in range(5):
                    total[o] = total[o] + value * weight[o][k]
            for o in range(5):
                merged[r + 4, o, part, :] = total[o].astype(BF)
        return carry

    hub_part((z + 2) % 4)
    hub_part((z + 1) % 4)
    g_core()
    hub_part((z + 3) % 4)
    hub_add((z + 2) % 4)
    send_a((z + 2) % 4)
    hub_part(z)
    hub_add((z + 1) % 4)
    send_a((z + 1) % 4)
    merged[0:4] = jnp.zeros((4, 5, TILE, TILE), BF)
    merged[20:24] = jnp.zeros((4, 5, TILE, TILE), BF)
    hub_add((z + 3) % 4)
    send_a((z + 3) % 4)
    lax.fori_loop(0, 4, merge, 0)
    hub_add(z)
    send_a(z)
    send_b(2)
    g_plane()
    lax.fori_loop(4, 8, merge, 0)
    send_b(1)
    lax.fori_loop(8, 12, merge, 0)
    send_b(3)
    g_z()
    lax.fori_loop(12, 16, merge, 0)
    for half, total in enumerate(collect(z)):
        sum_a[half] = total

    dsc[0:512, :] = jnp.zeros((512, WIDTH), BF)
    dsc[512 + ROWS :, :] = jnp.zeros((512, WIDTH), BF)

    def transposed(t):
        left = jnp.concatenate([merged[t + q, 4 - q] for q in range(5)], axis=0)
        right = dsc[pl.ds(pl.multiple_of(t * TILE, TILE), 5 * TILE), :]
        return lax.dot_general(left, right, TN, preferred_element_type=F32)

    for side, start in ((0, 0), (1, 18)):
        for i in range(2):
            rim_out[side, i * TILE : (i + 1) * TILE, :] = transposed(start + i).astype(BF)
    rim_low = remote(rim_out.at[0], rim_in.at[0], rim_s.at[0], rim_r.at[0], before)
    rim_high = remote(rim_out.at[1], rim_in.at[1], rim_s.at[1], rim_r.at[1], after)
    rim_low.start()
    rim_high.start()
    pending.extend((rim_low, rim_high))

    def interior(t, carry):
        here = rows_at(t * TILE, TILE)
        value = transposed(t + 2)
        value = value + lax.dot_general(dpre[here, :], ws[...], NT, preferred_element_type=F32)
        base[here, :] = value
        return carry

    lax.fori_loop(0, 4, interior, 0)
    send_c()
    lax.fori_loop(4, 16, interior, 0)
    g_gather()
    rim_low.wait_recv()
    rim_high.wait_recv()
    low = jnp.where(me == 0, 0.0, rim_in[1].astype(F32))
    base[:HALO, :] = base[:HALO, :] + low
    high = jnp.where(me == 127, 0.0, rim_in[0].astype(F32))
    base[ROWS - HALO :, :] = base[ROWS - HALO :, :] + high
    total = jnp.concatenate([hub_total(0), hub_total(1)], axis=1)
    upper = total.astype(BF)
    lower = (total - upper.astype(F32)).astype(BF)
    right = jnp.concatenate([upper, lower, jnp.zeros((64, WIDTH), BF)], axis=0)

    def finish(j, carry):
        here = rows_at(j * 256, 256)
        ids = lax.broadcasted_iota(I32, (256, TILE), 0) + j * 256
        place = (ids == hub_row).astype(F32).astype(BF)
        value = base[here, :] + jnp.dot(place, right, preferred_element_type=F32)
        fgrad[here, :] = value.astype(BF)
        return carry

    lax.fori_loop(0, 8, finish, 0)
    g_done()
    sums[...] = gall[...]
    for copy in pending:
        copy.wait_send()


def deliver(hid, fgrad, gall, hidden_out, grad_out, self_out, neighbor_out, bias_out, sem):
    copies = [pltpu.make_async_copy(hid, hidden_out, sem.at[0]), pltpu.make_async_copy(fgrad, grad_out, sem.at[1])]
    for copy in copies:
        copy.start()
    for which, out in ((0, self_out), (1, neighbor_out)):
        out[:, :TILE] = gall[which, :, :, 0:16, :].reshape(WIDTH, TILE)
        out[:, TILE:] = gall[which, :, :, 16:32, :].reshape(WIDTH, TILE)
    bias_out[:, :TILE] = gall[0, 0, 0, 32:33, :]
    bias_out[:, TILE:] = gall[0, 0, 0, 33:34, :]
    for copy in copies:
        copy.wait()


SCRATCH = [
    VMEM((TILES, TILE, WIDTH), BF),
    VMEM((6, TILE, WIDTH), BF),
    VMEM((6, TILE, WIDTH), BF),
    VMEM((TILES, SLOTS, TILE, TILE), I32),
    VMEM((ROWS, WIDTH), BF),
    VMEM((WIDTH, WIDTH), BF),
    VMEM((WIDTH, WIDTH), BF),
    VMEM((1, WIDTH), F32),
    VMEM((4, ROWS), I32),
    VMEM((4, ROWS), I32),
    VMEM((TILES, TILE), I32),
    VMEM((2, 4, 4, 4, 2, 32, TILE), BF),
    VMEM((HUBS, ROWS), BF),
    VMEM((4, ROWS), I32),
    VMEM((4, ROWS), I32),
    VMEM((4, 256, 512), BF),
    VMEM((24, 5, TILE, TILE), BF),
    VMEM((ROWS, WIDTH), F32),
    VMEM((ROWS, WIDTH), F32),
    VMEM((ROWS, TILE), F32),
    VMEM((ROWS, WIDTH), BF),
    VMEM((ROWS, WIDTH), BF),
    VMEM((ROWS + 1024, WIDTH), BF),
    VMEM((ROWS, WIDTH), F32),
    VMEM((2, HALO, WIDTH), BF),
    VMEM((2, HALO, WIDTH), BF),
    VMEM((4, 4, 4, 2, 32, WIDTH), BF),
    VMEM((4, 4, 4, 32, WIDTH), BF),
    VMEM((2, 4, 4, 4, 32, TILE), BF),
    VMEM((2, 3, 4, 4, 32, TILE), BF),
    VMEM((2, 4, 32, TILE), F32),
    VMEM((3, 2, 4, 32, TILE), BF),
    VMEM((3, 2, 4, 32, TILE), BF),
    VMEM((2, 4, 32, TILE), F32),
    VMEM((2, 3, 32, TILE), F32),
    VMEM((2, 4, 4, 40, TILE), F32),
    VMEM((4, 4, 40, TILE), F32),
    VMEM((4, 4, 40, TILE), F32),
    VMEM((15, 40, TILE), F32),
    VMEM((4, 40, TILE), F32),
    VMEM((2, 4, 4, 40, TILE), F32),
    DMA((8,)), DMA((TILES,)),
    DMA((2,)), DMA((2,)),
    DMA((2, 2, 3)), DMA((2, 2, 3)),
    DMA((2, 4, 3)), DMA((2, 4, 3)),
    DMA((8,)), DMA((8,)),
    DMA((2,)), DMA((2,)),
    DMA((4,)), DMA((4,)),
    DMA((2, 3, 4)), DMA((2, 3, 4)), DMA((3,)), DMA((3,)), DMA((2, 3)), DMA((2, 3)),
    DMA((1,)), DMA((1,)),
    DMA((15,)), DMA((15,)),
    DMA((3,)), DMA((3,)),
    DMA((15,)), DMA((15,)),
    DMA((1,)), DMA((1,)),
]


def local(
    features, self_weight, neighbor_weight, bias_term, tile_columns, tile_bits,
    hub_slots, hub_live, degree, hub_rows, cotangent,
):
    smem = pl.BlockSpec(memory_space=pltpu.SMEM)
    vmem = pl.BlockSpec(memory_space=VMEM)
    hbm = pl.BlockSpec(memory_space=pl.ANY)
    wide = jax.ShapeDtypeStruct((ROWS, WIDTH), BF)
    hidden, feature_grad, sums = pl.pallas_call(
        kernel,
        out_shape=(VMEM(wide.shape, BF), VMEM(wide.shape, BF), VMEM((2, 4, 4, 40, TILE), F32)),
        in_specs=[smem, smem] + [hbm] * 9,
        out_specs=(vmem, vmem, vmem),
        scratch_shapes=SCRATCH,
        name="sage_layer",
        compiler_params=pltpu.CompilerParams(
            collective_id=0, has_side_effects=True, vmem_limit_bytes=56 * 2**20
        ),
    )(
        tile_columns.T, hub_rows, features.reshape(TILES, TILE, WIDTH), tile_bits, cotangent, self_weight, neighbor_weight,
        bias_term.reshape(1, WIDTH), hub_slots.T, hub_live.T, degree.reshape(TILES, TILE),
    )
    square = jax.ShapeDtypeStruct((WIDTH, WIDTH), F32)
    hidden, feature_grad, self_grad, neighbor_grad, bias_grad = pl.pallas_call(
        deliver,
        out_shape=(wide, wide, square, square, jax.ShapeDtypeStruct((1, WIDTH), F32)),
        in_specs=[vmem, vmem, vmem],
        out_specs=(hbm, hbm, vmem, vmem, vmem),
        scratch_shapes=[DMA((2,))],
        compiler_params=pltpu.CompilerParams(vmem_limit_bytes=8 * 2**20),
        name="deliver",
    )(*(pltpu.with_memory_space_constraint(value, VMEM) for value in (hidden, feature_grad, sums)))
    return hidden, feature_grad, self_grad, neighbor_grad, bias_grad.reshape(WIDTH)


def solution(mesh):
    placed = (
        P("band", None), P(), P(), P(), P("band", None), P("band", None, None, None),
        P("band", None), P("band", None), P("band"), P("band"), P("band", None),
    )
    return jax.shard_map(
        local,
        mesh=mesh,
        in_specs=placed,
        out_specs=(P("band", None), P("band", None), P(), P(), P()),
        check_vma=False,
    )
```

```python
import math

import jax
import jax.numpy as jnp
from jax import lax
from jax.experimental import pallas as pl
from jax.experimental.pallas import tpu as pltpu
from jax.sharding import PartitionSpec as P

MESH = pl.DeviceIdType.MESH
BF = jnp.bfloat16
F32 = jnp.float32
I32 = jnp.int32
VMEM = pltpu.VMEM
DMA = pltpu.SemaphoreType.DMA

ROWS = 2048
WIDTH = 256
TILE = 128
TILES = 16
SLOTS = 6
HALO = 256
HUBS = 4096
ORDERS = ((0, 1, 2), (1, 2, 0))
PLANE = [(i, j) for i in range(4) for j in range(4) if (i, j) != (0, 0)]
TN = (((0,), (0,)), ((), ()))
NT = (((1,), (1,)), ((), ()))


def device(z, x, y, c):
    return ((z * 4 + x) * 4 + y) * 2 + c


def rows_at(start, size):
    return pl.ds(pl.multiple_of(start, size), size)


def remote(src, dst, send, recv, target):
    return pltpu.make_async_remote_copy(
        src_ref=src, dst_ref=dst, send_sem=send, recv_sem=recv, device_id=(target,), device_id_type=MESH
    )


def kernel(
    tcol, hrow, feat_hbm, bits_hbm, cot_hbm, ws_hbm, wn_hbm, bias_hbm, slots_hbm, live_hbm, deg_hbm,
    hid, fgrad, sums,
    feat, low, high, bits, cot, ws, wn, bias, slots, live, deg, table, counts, slot_low, slot_high, onehot, merged, band, pre0,
    rdeg, agg, dpre, dsc, base, rim_out, rim_in,
    hubp, hubc, hubs, recv_a, sum_a, out_b, recv_b, sum_b, recv_c,
    gpart, gcore, gsum, gsend, gxy, gz, gall,
    load_sem, bits_sem, halo_s, halo_r, ag_s, ag_r, line_s, line_r, core_s, core_r, rim_s, rim_r,
    hc_s, hc_r, ha_s, ha_r, hb_s, hb_r, hd_s, hd_r,
    gc_s, gc_r, gxy_s, gxy_r, gz_s, gz_r, gg_s, gg_r, gh_s, gh_r,
):
    me = lax.axis_index("band")
    z, x, y, c = me // 32, (me // 8) % 4, (me // 2) % 4, me % 2
    at = (z, x, y)
    partner = device(z, x, y, 1 - c)
    after, before = (me + 1) % 128, (me + 127) % 128

    def peer(dim, k):
        place = list(at)
        place[dim] = (place[dim] + k) % 4
        return tuple(place)

    load_f = pltpu.make_async_copy(feat_hbm, feat, load_sem.at[0])
    load_f.start()
    small = [
        pltpu.make_async_copy(source, target, load_sem.at[2 + i])
        for i, (source, target) in enumerate(
            ((slots_hbm, slots), (live_hbm, live), (ws_hbm, ws), (wn_hbm, wn), (bias_hbm, bias), (deg_hbm, deg))
        )
    ]
    barrier = pltpu.get_barrier_semaphore()
    greeted = [partner, after, before]
    greeted.extend(device(*peer(0, k), c) for k in (1, 2, 3))
    greeted.extend(device(z, (x + i) % 4, (y + j) % 4, c) for i, j in PLANE)
    for other in greeted:
        pl.semaphore_signal(barrier, inc=1, device_id=(other,), device_id_type=MESH)
    for load in small:
        load.start()
    load_c = pltpu.make_async_copy(cot_hbm, cot, load_sem.at[1])
    bit_loads = []
    for r in range(TILES):
        load = pltpu.make_async_copy(bits_hbm.at[r], bits.at[r], bits_sem.at[r])
        load.start()
        bit_loads.append(load)
    load_c.start()

    lane = lax.broadcasted_iota(I32, (32, TILE), 1)
    sub = lax.broadcasted_iota(I32, (32, TILE), 0)
    hub_col = jnp.full((32, TILE), -1, I32)
    hub_row = jnp.full((1, TILE), -1, I32)
    lane1 = lax.broadcasted_iota(I32, (1, TILE), 1)
    for h in range(32):
        value = hrow[h]
        hub_col = jnp.where(sub == h, value, hub_col)
        hub_row = jnp.where((lane1 == h) | (lane1 == h + 32), value, hub_row)
    pick = jnp.concatenate(
        [(hub_col == lane + j * TILE).astype(F32).astype(BF) for j in range(TILES)], axis=1
    )
    load_f.wait()
    own = jnp.dot(pick, feat[...].reshape(ROWS, WIDTH), preferred_element_type=F32).astype(BF)
    table[0, z, x, y, c] = own[:, :TILE]
    table[1, z, x, y, c] = own[:, TILE:]

    pl.semaphore_wait(barrier, len(greeted))

    def line(half, place, core, free):
        index = [half] + [slice(None) if d in free else place[d] for d in range(3)] + [core]
        return table.at[tuple(index)]

    pending = []

    def gather_send(phase, half):
        dim, free = ORDERS[half][phase], ORDERS[half][:phase]
        block = line(half, at, c, free)
        for k in (1, 3, 2):
            copy = remote(block, block, ag_s.at[phase, half, k - 1], ag_r.at[phase, half, k - 1], device(*peer(dim, k), c))
            copy.start()
            pending.append(copy)

    def gather_recv(phase, half, k):
        dim, free = ORDERS[half][phase], ORDERS[half][:phase]
        block = line(half, peer(dim, 4 - k), c, free)
        remote(block, block, ag_s.at[phase, half, k - 1], ag_r.at[phase, half, k - 1], device(*peer(dim, k), c)).wait_recv()

    def line_send(half, k):
        middle, last = ORDERS[half][1:]
        block = line(half, peer(middle, (4 - k) % 4), c, ORDERS[half][:1])
        for i in (1, 3, 2):
            copy = remote(block, block, line_s.at[half, k, i - 1], line_r.at[half, k, i - 1], device(*peer(last, i), c))
            copy.start()
            pending.append(copy)

    def line_recv(half, i):
        middle, last = ORDERS[half][1:]
        place = list(peer(last, 4 - i))
        for k in range(4):
            piece = list(place)
            piece[middle] = (piece[middle] + 4 - k) % 4
            block = line(half, piece, c, ORDERS[half][:1])
            remote(block, block, line_s.at[half, k, i - 1], line_r.at[half, k, i - 1], partner).wait_recv()
        return line(half, place, c, ORDERS[half][:2])

    def core_send(block, n):
        copy = remote(block, block, core_s.at[n], core_r.at[n], partner)
        copy.start()
        pending.append(copy)

    def core_recv(half, place, n):
        block = line(half, place, 1 - c, ORDERS[half][:2])
        remote(block, block, core_s.at[n], core_r.at[n], partner).wait_recv()

    gather_send(0, 0)
    gather_send(0, 1)

    for load in small:
        load.wait()
    named = jnp.where(live[...] == 1, slots[...], -1)
    slot_low[...] = named & 255
    slot_high[...] = named >> 8
    span = 512

    def build(j, carry):
        cols = rows_at(j * span, span)
        ids = lax.broadcasted_iota(I32, (256, span), 0).astype(jnp.int16)
        for k in range(4):
            value = jnp.broadcast_to(slot_low[k : k + 1, cols], (16, span)).astype(jnp.int16)
            value = jnp.broadcast_to(value[None], (16, 16, span)).reshape(256, span)
            onehot[k] = jnp.where(value == ids, jnp.ones((), BF), jnp.zeros((), BF))

        def block(h, carry):
            total = jnp.zeros((256, span), BF)
            for k in range(4):
                keep = jnp.broadcast_to(jnp.where(slot_high[k : k + 1, cols] == h, 1.0, 0.0), (16, span)).astype(BF)
                keep = jnp.broadcast_to(keep[None], (16, 16, span)).reshape(256, span)
                total = total + onehot[k] * keep
            counts[rows_at(h * 256, 256), cols] = total
            return carry

        return lax.fori_loop(0, HUBS // 256, block, carry)

    lax.fori_loop(0, 2, build, 0)
    for half in range(2):
        for k in (1, 3, 2):
            gather_recv(0, half, k)
        gather_send(1, half)
        line_send(half, 0)
    lax.fori_loop(2, 4, build, 0)
    for k in (1, 3, 2):
        for half in range(2):
            gather_recv(1, half, k)
            line_send(half, k)
    halo_low = remote(feat.at[0:2], high.at[4:6], halo_s.at[0], halo_r.at[0], before)
    halo_high = remote(feat.at[14:16], low.at[0:2], halo_s.at[1], halo_r.at[1], after)
    halo_low.start()
    halo_high.start()
    pending.extend((halo_low, halo_high))
    for half in range(2):
        core_send(line(half, at, c, ORDERS[half][:2]), half)

    def own_term(j, carry):
        here = rows_at(j * 256, 256)
        pre0[here, :] = jnp.dot(feat[pl.ds(j * 2, 2)].reshape(256, WIDTH), ws[...], preferred_element_type=F32) + bias[...]
        return carry

    def divide(r, carry):
        row = 1.0 / deg[pl.ds(r, 1), :].astype(F32)
        rdeg[rows_at(r * TILE, TILE), :] = jnp.broadcast_to(row, (TILE, TILE)).T
        return carry

    def forward(rows, first):
        def body(r, carry):
            pltpu.make_async_copy(bits_hbm.at[r], bits.at[r], bits_sem.at[r]).wait()
            left = jnp.concatenate([bits[r, k].astype(F32).astype(BF) for k in range(SLOTS)], axis=1)
            right = jnp.concatenate([rows[jnp.clip(tcol[k, r] - first, 0, rows.shape[0] - 1)] for k in range(SLOTS)], axis=0)
            band[rows_at(r * TILE, TILE), :] = jnp.dot(left, right, preferred_element_type=F32)
            return carry

        return body

    lax.fori_loop(0, 8, own_term, 0)
    lax.fori_loop(0, TILES, divide, 0)
    lax.fori_loop(2, 8, forward(feat, 2), 0)
    n = 2
    for k in (1, 3):
        for half in range(2):
            core_send(line_recv(half, k), n)
            n += 1
    lax.fori_loop(8, 14, forward(feat, 2), 0)
    for half in range(2):
        core_send(line_recv(half, 2), n)
        n += 1
    low[2:6] = feat[0:4]
    high[0:4] = feat[12:16]
    halo_low.wait_recv()
    halo_high.wait_recv()
    low[0:2] = jnp.where(me == 0, 0.0, low[0:2].astype(F32)).astype(BF)
    high[4:6] = jnp.where(me == 127, 0.0, high[4:6].astype(F32)).astype(BF)
    lax.fori_loop(0, 2, forward(low, 0), 0)
    lax.fori_loop(14, 16, forward(high, 14), 0)

    n = 0
    for k in (0, 1, 3, 2):
        for half in range(2):
            core_recv(half, peer(ORDERS[half][2], (4 - k) % 4), n)
            n += 1

    early = len(pending)

    load_c.wait()

    def layer(j, carry):
        cols = rows_at(j * 1024, 1024)
        right = jnp.concatenate([table[0].reshape(HUBS, TILE), table[1].reshape(HUBS, TILE)], axis=1)
        base[cols, :] = lax.dot_general(counts[:, cols], right, TN, preferred_element_type=F32)

        def chunk(i, carry):
            start = j * 1024 + i * 256
            here = rows_at(start, 256)
            for s in range(4):
                part = rows_at(start + s * 64, 64)
                scale = rdeg[part, :]
                total = band[part, :] + base[part, :]
                agg[part, :] = (total * jnp.concatenate([scale, scale], axis=1)).astype(BF)
            pre = pre0[here, :] + jnp.dot(agg[here, :], wn[...], preferred_element_type=F32)
            for s in range(4):
                part = rows_at(start + s * 64, 64)
                v = pre[s * 64 : s * 64 + 64, :]
                sig = 1.0 / (1.0 + jnp.exp(-v))
                act = v * sig
                hid[part, :] = act.astype(BF)
                dpre[part, :] = (cot[part, :].astype(F32) * sig * (1.0 + v - act)).astype(BF)
            back = lax.dot_general(dpre[here, :], wn[...], NT, preferred_element_type=F32)
            scale = rdeg[here, :]
            dsc[rows_at(512 + start, 256), :] = (back * jnp.concatenate([scale, scale], axis=1)).astype(BF)
            return carry

        return lax.fori_loop(0, 4, chunk, carry)

    lax.fori_loop(0, 2, layer, 0)

    gpart[:, :, :, 32:40, :] = jnp.zeros((2, 4, 4, 8, TILE), F32)
    for which, left in ((0, feat[...].reshape(ROWS, WIDTH)), (1, agg[...])):
        part = lax.dot_general(left, dpre[...], TN, preferred_element_type=F32).reshape(4, 4, 16, WIDTH)
        gpart[which, :, :, 0:16, :] = part[..., :TILE]
        gpart[which, :, :, 16:32, :] = part[..., TILE:]
    part = jnp.dot(jnp.ones((16, ROWS), BF), dpre[...], preferred_element_type=F32)
    row8 = lax.broadcasted_iota(I32, (8, TILE), 0)
    gpart[0, 0, 0, 32:40, :] = jnp.where(row8 == 0, part[:8, :TILE], jnp.where(row8 == 1, part[:8, TILE:], 0.0))
    copy_gc = remote(gpart.at[1 - c], gcore, gc_s.at[0], gc_r.at[0], partner)
    copy_gc.start()
    pending.append(copy_gc)

    def plane(n):
        return (x + n // 4) % 4, (y + n % 4) % 4

    def g_core():
        copy_gc.wait_recv()
        total = gpart[c] + gcore[...]
        gsum[...] = total
        gsend[...] = jnp.concatenate([total, jnp.zeros((4, 4, 8, TILE), F32)], axis=2).astype(BF)

        def send(n, carry):
            px, py = plane(n)
            remote(gsend.at[py, px], gxy.at[n], gxy_s.at[n], gxy_r.at[n], device(z, px, py, c)).start()
            return carry

        lax.fori_loop(1, 16, send, 0)

    def g_plane():
        def add(n, total):
            remote(gsend.at[y, x], gxy.at[n], gxy_s.at[n], gxy_r.at[n], partner).wait_recv()
            return total + gxy[n, 0:40, :].astype(F32)

        gz[z] = lax.fori_loop(1, 16, add, gsum[y, x])
        for k in (1, 3, 2):
            copy = remote(gz.at[z], gz.at[z], gz_s.at[k - 1], gz_r.at[k - 1], device(*peer(0, k), c))
            copy.start()
            pending.append(copy)

    def g_z():
        for k in (1, 2, 3):
            slot = gz.at[(z + 4 - k) % 4]
            remote(slot, slot, gz_s.at[k - 1], gz_r.at[k - 1], partner).wait_recv()
        total = (gz[0] + gz[1] + gz[2] + gz[3]) * (1.0 / 512.0)
        gall[c, y, x] = jnp.concatenate([total, jnp.zeros((8, TILE), F32)], axis=0).astype(BF)
        piece = gall.at[c, y, x]

        def send(n, carry):
            px, py = plane(n)
            remote(piece, piece, gg_s.at[n], gg_r.at[n], device(z, px, py, c)).start()
            return carry

        lax.fori_loop(1, 16, send, 0)

    def g_gather():
        def wait(n, carry):
            slot = gall.at[c, (y + 4 - n % 4) % 4, (x + 4 - n // 4) % 4]
            remote(slot, slot, gg_s.at[n], gg_r.at[n], partner).wait_recv()
            return carry

        lax.fori_loop(1, 16, wait, 0)
        piece = gall.at[c]
        copy = remote(piece, piece, gh_s.at[0], gh_r.at[0], partner)
        copy.start()
        pending.append(copy)

    def g_done():
        slot = gall.at[1 - c]
        remote(slot, slot, gh_s.at[0], gh_r.at[0], partner).wait_recv()

    def hub_part(zc):
        left = counts[rows_at(zc * 1024, 1024), :]
        value = jnp.dot(left, dsc[512 : 512 + ROWS, :], preferred_element_type=F32)
        hubp[zc] = value.astype(BF).reshape(4, 4, 2, 32, WIDTH)
        remote(hubp.at[zc, :, :, 1 - c], hubc.at[zc], hc_s.at[zc], hc_r.at[zc], partner).start()

    def hub_add(zc):
        remote(hubp.at[zc, :, :, 1 - c], hubc.at[zc], hc_s.at[zc], hc_r.at[zc], partner).wait_recv()
        for i in range(4):
            total = (hubp[zc, i, :, c].astype(F32) + hubc[zc, i].astype(F32)).astype(BF)
            hubs[0, zc, i] = total[..., :TILE]
            hubs[1, zc, i] = total[..., TILE:]

    def send_a(zc):
        for k in (2, 1, 3):
            for half in range(2):
                source = hubs.at[0, zc, (x + k) % 4] if half == 0 else hubs.at[1, zc, :, (y + k) % 4]
                remote(
                    source, recv_a.at[half, k - 1, zc], ha_s.at[half, k - 1, zc], ha_r.at[half, k - 1, zc],
                    device(*peer(1 + half, k), c),
                ).start()

    def collect(zc):
        for k in range(3):
            for half in range(2):
                block = recv_a.at[half, k, zc]
                remote(block, block, ha_s.at[half, k, zc], ha_r.at[half, k, zc], partner).wait_recv()
        totals = []
        for half in range(2):
            total = (hubs[0, zc, x] if half == 0 else hubs[1, zc, :, y]).astype(F32)
            for k in range(3):
                total = total + recv_a[half, k, zc].astype(F32)
            totals.append(total)
        return totals

    def send_b(k):
        for half, total in enumerate(collect((z + k) % 4)):
            out_b[k - 1, half] = total.astype(BF)
        remote(out_b.at[k - 1], recv_b.at[k - 1], hb_s.at[k - 1], hb_r.at[k - 1], device(*peer(0, k), c)).start()

    def send_c():
        for k in range(3):
            remote(recv_b.at[k], recv_b.at[k], hb_s.at[k], hb_r.at[k], partner).wait_recv()
        for half in range(2):
            total = sum_a[half]
            for k in range(3):
                total = total + recv_b[k, half].astype(F32)
            sum_b[half] = total
        for k in (2, 1, 3):
            for half, dim in ((0, 2), (1, 1)):
                copy = remote(
                    sum_b.at[half, (at[dim] + k) % 4], recv_c.at[half, k - 1],
                    hd_s.at[half, k - 1], hd_r.at[half, k - 1], device(*peer(dim, k), c),
                )
                copy.start()
                pending.append(copy)

    def hub_total(half):
        for k in range(3):
            remote(recv_c.at[half, k], recv_c.at[half, k], hd_s.at[half, k], hd_r.at[half, k], partner).wait_recv()
        return sum_b[half, at[2 - half]] + recv_c[half, 0] + recv_c[half, 1] + recv_c[half, 2]

    def merge(r, carry):
        weight = [[(tcol[k, r] == r + o).astype(F32) for k in range(SLOTS)] for o in range(5)]
        for s in range(4):
            part = pl.ds(s * 32, 32)
            total = [jnp.zeros((32, TILE), F32) for _ in range(5)]
            for k in range(SLOTS):
                value = bits[r, k, part, :].astype(F32)
                for o in range(5):
                    total[o] = total[o] + value * weight[o][k]
            for o in range(5):
                merged[r + 4, o, part, :] = total[o].astype(BF)
        return carry

    def order(i):
        return jnp.where(i == 0, 2, jnp.where(i == 1, 1, jnp.where(i == 2, 3, 0)))

    merged[0:4] = jnp.zeros((4, 5, TILE, TILE), BF)
    merged[20:24] = jnp.zeros((4, 5, TILE, TILE), BF)

    def step(i, carry):
        @pl.when(i < 4)
        def _():
            hub_part((z + order(i)) % 4)

        @pl.when(i == 1)
        def _():
            g_core()

        @pl.when(i >= 4)
        def _():
            lax.fori_loop((i - 4) * 4, (i - 3) * 4, merge, 0)

        @pl.when(i >= 2)
        def _():
            zc = (z + order(i - 2)) % 4
            hub_add(zc)
            send_a(zc)

        return carry

    lax.fori_loop(0, 6, step, 0)
    g_plane()

    def step_b(i, carry):
        lax.fori_loop(8 + i * 2, 10 + i * 2, merge, 0)
        send_b(order(i))
        return carry

    lax.fori_loop(0, 3, step_b, 0)
    g_z()
    lax.fori_loop(14, 16, merge, 0)
    for half, total in enumerate(collect(z)):
        sum_a[half] = total

    dsc[0:512, :] = jnp.zeros((512, WIDTH), BF)
    dsc[512 + ROWS :, :] = jnp.zeros((512, WIDTH), BF)

    def transposed(t):
        left = jnp.concatenate([merged[t + q, 4 - q] for q in range(5)], axis=0)
        right = dsc[pl.ds(pl.multiple_of(t * TILE, TILE), 5 * TILE), :]
        return lax.dot_general(left, right, TN, preferred_element_type=F32)

    for side, start in ((0, 0), (1, 18)):
        for i in range(2):
            rim_out[side, i * TILE : (i + 1) * TILE, :] = transposed(start + i).astype(BF)
    rim_low = remote(rim_out.at[0], rim_in.at[0], rim_s.at[0], rim_r.at[0], before)
    rim_high = remote(rim_out.at[1], rim_in.at[1], rim_s.at[1], rim_r.at[1], after)
    rim_low.start()
    rim_high.start()
    pending.extend((rim_low, rim_high))

    def interior(t, carry):
        here = rows_at(t * TILE, TILE)
        value = transposed(t + 2)
        value = value + lax.dot_general(dpre[here, :], ws[...], NT, preferred_element_type=F32)
        base[here, :] = value
        return carry

    lax.fori_loop(0, 4, interior, 0)
    send_c()
    lax.fori_loop(4, 16, interior, 0)
    g_gather()
    rim_low.wait_recv()
    rim_high.wait_recv()
    low = jnp.where(me == 0, 0.0, rim_in[1].astype(F32))
    base[:HALO, :] = base[:HALO, :] + low
    high = jnp.where(me == 127, 0.0, rim_in[0].astype(F32))
    base[ROWS - HALO :, :] = base[ROWS - HALO :, :] + high
    for copy in pending[:early]:
        copy.wait_send()

    def sent_parts(zc, carry):
        remote(hubc.at[zc], hubc.at[zc], hc_s.at[zc], hc_r.at[zc], partner).wait_send()
        for k in range(3):
            for half in range(2):
                block = recv_a.at[half, k, zc]
                remote(block, block, ha_s.at[half, k, zc], ha_r.at[half, k, zc], partner).wait_send()
        return carry

    def sent_plane(n, carry):
        remote(gsend.at[y, x], gxy.at[n], gxy_s.at[n], gxy_r.at[n], partner).wait_send()
        return carry

    lax.fori_loop(0, 4, sent_parts, 0)
    lax.fori_loop(1, 16, sent_plane, 0)
    for k in range(3):
        remote(recv_b.at[k], recv_b.at[k], hb_s.at[k], hb_r.at[k], partner).wait_send()
    total = jnp.concatenate([hub_total(0), hub_total(1)], axis=1)
    upper = total.astype(BF)
    lower = (total - upper.astype(F32)).astype(BF)
    right = jnp.concatenate([upper, lower, jnp.zeros((64, WIDTH), BF)], axis=0)

    def finish(j, carry):
        here = rows_at(j * 256, 256)
        ids = lax.broadcasted_iota(I32, (256, TILE), 0) + j * 256
        place = (ids == hub_row).astype(F32).astype(BF)
        value = base[here, :] + jnp.dot(place, right, preferred_element_type=F32)
        fgrad[here, :] = value.astype(BF)
        return carry

    lax.fori_loop(0, 8, finish, 0)
    g_done()
    sums[...] = gall[...]
    for copy in pending[early:]:
        copy.wait_send()

    def sent_gather(n, carry):
        remote(gall.at[c, y, x], gall.at[c, y, x], gg_s.at[n], gg_r.at[n], partner).wait_send()
        return carry

    lax.fori_loop(1, 16, sent_gather, 0)


def deliver(hid, fgrad, gall, hidden_out, grad_out, self_out, neighbor_out, bias_out, sem):
    copies = [pltpu.make_async_copy(hid, hidden_out, sem.at[0]), pltpu.make_async_copy(fgrad, grad_out, sem.at[1])]
    for copy in copies:
        copy.start()
    for which, out in ((0, self_out), (1, neighbor_out)):
        out[:, :TILE] = gall[which, :, :, 0:16, :].astype(F32).reshape(WIDTH, TILE)
        out[:, TILE:] = gall[which, :, :, 16:32, :].astype(F32).reshape(WIDTH, TILE)
    bias_row = gall[0, 0, 0, 32:40, :].astype(F32)
    bias_out[:, :TILE] = bias_row[0:1, :]
    bias_out[:, TILE:] = bias_row[1:2, :]
    for copy in copies:
        copy.wait()


SCRATCH = [
    VMEM((TILES, TILE, WIDTH), BF),
    VMEM((6, TILE, WIDTH), BF),
    VMEM((6, TILE, WIDTH), BF),
    VMEM((TILES, SLOTS, TILE, TILE), I32),
    VMEM((ROWS, WIDTH), BF),
    VMEM((WIDTH, WIDTH), BF),
    VMEM((WIDTH, WIDTH), BF),
    VMEM((1, WIDTH), F32),
    VMEM((4, ROWS), I32),
    VMEM((4, ROWS), I32),
    VMEM((TILES, TILE), I32),
    VMEM((2, 4, 4, 4, 2, 32, TILE), BF),
    VMEM((HUBS, ROWS), BF),
    VMEM((4, ROWS), I32),
    VMEM((4, ROWS), I32),
    VMEM((4, 256, 512), BF),
    VMEM((24, 5, TILE, TILE), BF),
    VMEM((ROWS, WIDTH), F32),
    VMEM((ROWS, WIDTH), F32),
    VMEM((ROWS, TILE), F32),
    VMEM((ROWS, WIDTH), BF),
    VMEM((ROWS, WIDTH), BF),
    VMEM((ROWS + 1024, WIDTH), BF),
    VMEM((ROWS, WIDTH), F32),
    VMEM((2, HALO, WIDTH), BF),
    VMEM((2, HALO, WIDTH), BF),
    VMEM((4, 4, 4, 2, 32, WIDTH), BF),
    VMEM((4, 4, 4, 32, WIDTH), BF),
    VMEM((2, 4, 4, 4, 32, TILE), BF),
    VMEM((2, 3, 4, 4, 32, TILE), BF),
    VMEM((2, 4, 32, TILE), F32),
    VMEM((3, 2, 4, 32, TILE), BF),
    VMEM((3, 2, 4, 32, TILE), BF),
    VMEM((2, 4, 32, TILE), F32),
    VMEM((2, 3, 32, TILE), F32),
    VMEM((2, 4, 4, 40, TILE), F32),
    VMEM((4, 4, 40, TILE), F32),
    VMEM((4, 4, 40, TILE), F32),
    VMEM((4, 4, 48, TILE), BF),
    VMEM((16, 48, TILE), BF),
    VMEM((4, 40, TILE), F32),
    VMEM((2, 4, 4, 48, TILE), BF),
    DMA((8,)), DMA((TILES,)),
    DMA((2,)), DMA((2,)),
    DMA((2, 2, 3)), DMA((2, 2, 3)),
    DMA((2, 4, 3)), DMA((2, 4, 3)),
    DMA((8,)), DMA((8,)),
    DMA((2,)), DMA((2,)),
    DMA((4,)), DMA((4,)),
    DMA((2, 3, 4)), DMA((2, 3, 4)), DMA((3,)), DMA((3,)), DMA((2, 3)), DMA((2, 3)),
    DMA((1,)), DMA((1,)),
    DMA((16,)), DMA((16,)),
    DMA((3,)), DMA((3,)),
    DMA((16,)), DMA((16,)),
    DMA((1,)), DMA((1,)),
]


def local(
    features, self_weight, neighbor_weight, bias_term, tile_columns, tile_bits,
    hub_slots, hub_live, degree, hub_rows, cotangent,
):
    smem = pl.BlockSpec(memory_space=pltpu.SMEM)
    vmem = pl.BlockSpec(memory_space=VMEM)
    hbm = pl.BlockSpec(memory_space=pl.ANY)
    wide = jax.ShapeDtypeStruct((ROWS, WIDTH), BF)
    hidden, feature_grad, sums = pl.pallas_call(
        kernel,
        out_shape=(VMEM(wide.shape, BF), VMEM(wide.shape, BF), VMEM((2, 4, 4, 48, TILE), BF)),
        in_specs=[smem, smem] + [hbm] * 9,
        out_specs=(vmem, vmem, vmem),
        scratch_shapes=SCRATCH,
        name="sage_layer",
        compiler_params=pltpu.CompilerParams(
            collective_id=0, has_side_effects=True, vmem_limit_bytes=56 * 2**20
        ),
    )(
        tile_columns.T, hub_rows, features.reshape(TILES, TILE, WIDTH), tile_bits, cotangent, self_weight, neighbor_weight,
        bias_term.reshape(1, WIDTH), hub_slots.T, hub_live.T, degree.reshape(TILES, TILE),
    )
    square = jax.ShapeDtypeStruct((WIDTH, WIDTH), F32)
    hidden, feature_grad, self_grad, neighbor_grad, bias_grad = pl.pallas_call(
        deliver,
        out_shape=(wide, wide, square, square, jax.ShapeDtypeStruct((1, WIDTH), F32)),
        in_specs=[vmem, vmem, vmem],
        out_specs=(hbm, hbm, vmem, vmem, vmem),
        scratch_shapes=[DMA((2,))],
        compiler_params=pltpu.CompilerParams(vmem_limit_bytes=8 * 2**20),
        name="deliver",
    )(*(pltpu.with_memory_space_constraint(value, VMEM) for value in (hidden, feature_grad, sums)))
    return hidden, feature_grad, self_grad, neighbor_grad, bias_grad.reshape(WIDTH)


def solution(mesh):
    placed = (
        P("band", None), P(), P(), P(), P("band", None), P("band", None, None, None),
        P("band", None), P("band", None), P("band"), P("band"), P("band", None),
    )
    return jax.shard_map(
        local,
        mesh=mesh,
        in_specs=placed,
        out_specs=(P("band", None), P("band", None), P(), P(), P()),
        check_vma=False,
    )
```

```python
import math

import jax
import jax.numpy as jnp
from jax import lax
from jax.experimental import pallas as pl
from jax.experimental.pallas import tpu as pltpu
from jax.sharding import PartitionSpec as P

MESH = pl.DeviceIdType.MESH
BF = jnp.bfloat16
F32 = jnp.float32
I32 = jnp.int32
VMEM = pltpu.VMEM
DMA = pltpu.SemaphoreType.DMA

ROWS = 2048
WIDTH = 256
TILE = 128
TILES = 16
SLOTS = 6
HALO = 256
HUBS = 4096
ORDERS = ((0, 1, 2), (1, 2, 0))
PLANE = [(i, j) for i in range(4) for j in range(4) if (i, j) != (0, 0)]
TN = (((0,), (0,)), ((), ()))
NT = (((1,), (1,)), ((), ()))


def device(z, x, y, c):
    return ((z * 4 + x) * 4 + y) * 2 + c


def rows_at(start, size):
    return pl.ds(pl.multiple_of(start, size), size)


def remote(src, dst, send, recv, target):
    return pltpu.make_async_remote_copy(
        src_ref=src, dst_ref=dst, send_sem=send, recv_sem=recv, device_id=(target,), device_id_type=MESH
    )


def kernel(
    tcol, hrow, feat_hbm, bits_hbm, cot_hbm, ws_hbm, wn_hbm, bias_hbm, slots_hbm, live_hbm, deg_hbm,
    hid, fgrad, sums,
    feat, low, high, bits, cot, ws, wn, bias, slots, live, deg, table, counts, slot_low, slot_high, onehot, merged, band, pre0,
    rdeg, agg, dpre, dsc, base, rim_out, rim_in,
    hubp, hubc, hubs, recv_a, sum_a, out_b, recv_b, sum_b, recv_c,
    gpart, gcore, gsum, gsend, gxy, gz, gall,
    load_sem, feat_sem, bits_sem, halo_s, halo_r, ag_s, ag_r, line_s, line_r, core_s, core_r, rim_s, rim_r,
    hc_s, hc_r, ha_s, ha_r, hb_s, hb_r, hd_s, hd_r,
    gc_s, gc_r, gxy_s, gxy_r, gz_s, gz_r, gg_s, gg_r, gh_s, gh_r,
):
    me = lax.axis_index("band")
    z, x, y, c = me // 32, (me // 8) % 4, (me // 2) % 4, me % 2
    at = (z, x, y)
    partner = device(z, x, y, 1 - c)
    after, before = (me + 1) % 128, (me + 127) % 128

    def peer(dim, k):
        place = list(at)
        place[dim] = (place[dim] + k) % 4
        return tuple(place)

    load_f = [
        pltpu.make_async_copy(feat_hbm.at[q * 4 : q * 4 + 4], feat.at[q * 4 : q * 4 + 4], feat_sem.at[q]) for q in range(4)
    ]
    for load in load_f:
        load.start()
    small = [
        pltpu.make_async_copy(source, target, load_sem.at[2 + i])
        for i, (source, target) in enumerate(
            ((slots_hbm, slots), (live_hbm, live), (ws_hbm, ws), (wn_hbm, wn), (bias_hbm, bias), (deg_hbm, deg))
        )
    ]
    barrier = pltpu.get_barrier_semaphore()
    greeted = [partner, after, before]
    greeted.extend(device(*peer(0, k), c) for k in (1, 2, 3))
    greeted.extend(device(z, (x + i) % 4, (y + j) % 4, c) for i, j in PLANE)
    for other in greeted:
        pl.semaphore_signal(barrier, inc=1, device_id=(other,), device_id_type=MESH)
    for load in small:
        load.start()
    load_c = pltpu.make_async_copy(cot_hbm, cot, load_sem.at[1])
    bit_loads = []
    for r in range(TILES):
        load = pltpu.make_async_copy(bits_hbm.at[r], bits.at[r], bits_sem.at[r])
        bit_loads.append(load)

    lane = lax.broadcasted_iota(I32, (32, TILE), 1)
    sub = lax.broadcasted_iota(I32, (32, TILE), 0)
    hub_col = jnp.full((32, TILE), -1, I32)
    hub_row = jnp.full((1, TILE), -1, I32)
    lane1 = lax.broadcasted_iota(I32, (1, TILE), 1)
    for h in range(32):
        value = hrow[h]
        hub_col = jnp.where(sub == h, value, hub_col)
        hub_row = jnp.where((lane1 == h) | (lane1 == h + 32), value, hub_row)
    pick = jnp.concatenate(
        [(hub_col == lane + j * TILE).astype(F32).astype(BF) for j in range(TILES)], axis=1
    )
    own = jnp.zeros((32, WIDTH), F32)
    for q in range(4):
        load_f[q].wait()
        rows = feat[q * 4 : q * 4 + 4].reshape(512, WIDTH)
        own = own + jnp.dot(pick[:, q * 512 : q * 512 + 512], rows, preferred_element_type=F32)
    own = own.astype(BF)
    table[0, z, x, y, c] = own[:, :TILE]
    table[1, z, x, y, c] = own[:, TILE:]

    pl.semaphore_wait(barrier, len(greeted))

    def line(half, place, core, free):
        index = [half] + [slice(None) if d in free else place[d] for d in range(3)] + [core]
        return table.at[tuple(index)]

    pending = []

    def gather_send(phase, half):
        dim, free = ORDERS[half][phase], ORDERS[half][:phase]
        block = line(half, at, c, free)
        for k in (1, 3, 2):
            copy = remote(block, block, ag_s.at[phase, half, k - 1], ag_r.at[phase, half, k - 1], device(*peer(dim, k), c))
            copy.start()
            pending.append(copy)

    def gather_recv(phase, half, k):
        dim, free = ORDERS[half][phase], ORDERS[half][:phase]
        block = line(half, peer(dim, 4 - k), c, free)
        remote(block, block, ag_s.at[phase, half, k - 1], ag_r.at[phase, half, k - 1], device(*peer(dim, k), c)).wait_recv()

    def line_send(half, k):
        middle, last = ORDERS[half][1:]
        block = line(half, peer(middle, (4 - k) % 4), c, ORDERS[half][:1])
        for i in (1, 3, 2):
            copy = remote(block, block, line_s.at[half, k, i - 1], line_r.at[half, k, i - 1], device(*peer(last, i), c))
            copy.start()
            pending.append(copy)

    def line_recv(half, i):
        middle, last = ORDERS[half][1:]
        place = list(peer(last, 4 - i))
        for k in range(4):
            piece = list(place)
            piece[middle] = (piece[middle] + 4 - k) % 4
            block = line(half, piece, c, ORDERS[half][:1])
            remote(block, block, line_s.at[half, k, i - 1], line_r.at[half, k, i - 1], partner).wait_recv()
        return line(half, place, c, ORDERS[half][:2])

    def core_send(block, n):
        copy = remote(block, block, core_s.at[n], core_r.at[n], partner)
        copy.start()
        pending.append(copy)

    def core_recv(half, place, n):
        block = line(half, place, 1 - c, ORDERS[half][:2])
        remote(block, block, core_s.at[n], core_r.at[n], partner).wait_recv()

    gather_send(0, 0)
    gather_send(0, 1)
    for load in bit_loads:
        load.start()
    load_c.start()

    for load in small:
        load.wait()
    named = jnp.where(live[...] == 1, slots[...], -1)
    slot_low[...] = named & 255
    slot_high[...] = named >> 8
    span = 512

    def build(j, carry):
        cols = rows_at(j * span, span)
        ids = lax.broadcasted_iota(I32, (256, span), 0).astype(jnp.int16)
        for k in range(4):
            value = jnp.broadcast_to(slot_low[k : k + 1, cols], (16, span)).astype(jnp.int16)
            value = jnp.broadcast_to(value[None], (16, 16, span)).reshape(256, span)
            onehot[k] = jnp.where(value == ids, jnp.ones((), BF), jnp.zeros((), BF))

        def block(h, carry):
            total = jnp.zeros((256, span), BF)
            for k in range(4):
                keep = jnp.broadcast_to(jnp.where(slot_high[k : k + 1, cols] == h, 1.0, 0.0), (16, span)).astype(BF)
                keep = jnp.broadcast_to(keep[None], (16, 16, span)).reshape(256, span)
                total = total + onehot[k] * keep
            counts[h // 4, pl.ds((h % 4) * 4, 4), :, :, cols] = total.reshape(4, 2, 32, span)
            return carry

        return lax.fori_loop(0, HUBS // 256, block, carry)

    lax.fori_loop(0, 2, build, 0)
    for half in range(2):
        for k in (1, 3, 2):
            gather_recv(0, half, k)
        gather_send(1, half)
        line_send(half, 0)
    lax.fori_loop(2, 4, build, 0)
    for k in (1, 3, 2):
        for half in range(2):
            gather_recv(1, half, k)
            line_send(half, k)
    halo_low = remote(feat.at[0:2], high.at[4:6], halo_s.at[0], halo_r.at[0], before)
    halo_high = remote(feat.at[14:16], low.at[0:2], halo_s.at[1], halo_r.at[1], after)
    halo_low.start()
    halo_high.start()
    pending.extend((halo_low, halo_high))
    for half in range(2):
        core_send(line(half, at, c, ORDERS[half][:2]), half)

    def own_term(j, carry):
        here = rows_at(j * 256, 256)
        pre0[here, :] = jnp.dot(feat[pl.ds(j * 2, 2)].reshape(256, WIDTH), ws[...], preferred_element_type=F32) + bias[...]
        return carry

    def divide(r, carry):
        row = 1.0 / deg[pl.ds(r, 1), :].astype(F32)
        rdeg[rows_at(r * TILE, TILE), :] = jnp.broadcast_to(row, (TILE, TILE)).T
        return carry

    def forward(rows, first):
        def body(r, carry):
            pltpu.make_async_copy(bits_hbm.at[r], bits.at[r], bits_sem.at[r]).wait()
            left = jnp.concatenate([bits[r, k].astype(F32).astype(BF) for k in range(SLOTS)], axis=1)
            right = jnp.concatenate([rows[jnp.clip(tcol[k, r] - first, 0, rows.shape[0] - 1)] for k in range(SLOTS)], axis=0)
            band[rows_at(r * TILE, TILE), :] = jnp.dot(left, right, preferred_element_type=F32)
            return carry

        return body

    lax.fori_loop(0, 8, own_term, 0)
    lax.fori_loop(0, TILES, divide, 0)
    lax.fori_loop(2, 8, forward(feat, 2), 0)
    n = 2
    for k in (1, 3):
        for half in range(2):
            core_send(line_recv(half, k), n)
            n += 1
    lax.fori_loop(8, 14, forward(feat, 2), 0)
    for half in range(2):
        core_send(line_recv(half, 2), n)
        n += 1

    def hub_terms(core, add):
        def nodes(j, carry):
            cols = rows_at(j * 1024, 1024)
            right = jnp.concatenate([table[half, :, :, :, core].reshape(HUBS // 2, TILE) for half in range(2)], axis=1)
            left = counts[:, :, core, :, cols].reshape(HUBS // 2, 1024)
            value = lax.dot_general(left, right, TN, preferred_element_type=F32)
            base[cols, :] = base[cols, :] + value if add else value
            return carry

        lax.fori_loop(0, 2, nodes, 0)

    hub_terms(c, False)
    low[2:6] = feat[0:4]
    high[0:4] = feat[12:16]
    halo_low.wait_recv()
    halo_high.wait_recv()
    low[0:2] = jnp.where(me == 0, 0.0, low[0:2].astype(F32)).astype(BF)
    high[4:6] = jnp.where(me == 127, 0.0, high[4:6].astype(F32)).astype(BF)
    lax.fori_loop(0, 2, forward(low, 0), 0)
    lax.fori_loop(14, 16, forward(high, 14), 0)

    n = 0
    for k in (0, 1, 3, 2):
        for half in range(2):
            core_recv(half, peer(ORDERS[half][2], (4 - k) % 4), n)
            n += 1

    early = len(pending)

    load_c.wait()

    def layer(i, carry):
        start = i * 512
        here = rows_at(start, 512)
        for s in range(8):
            part = rows_at(start + s * 64, 64)
            scale = rdeg[part, :]
            total = band[part, :] + base[part, :]
            agg[part, :] = (total * jnp.concatenate([scale, scale], axis=1)).astype(BF)
        pre = pre0[here, :] + jnp.dot(agg[here, :], wn[...], preferred_element_type=F32)
        for s in range(8):
            part = rows_at(start + s * 64, 64)
            v = pre[s * 64 : s * 64 + 64, :]
            sig = 0.5 * jnp.tanh(0.5 * v) + 0.5
            act = v * sig
            hid[part, :] = act.astype(BF)
            dpre[part, :] = (cot[part, :].astype(F32) * sig * (1.0 + v - act)).astype(BF)
        back = lax.dot_general(dpre[here, :], wn[...], NT, preferred_element_type=F32)
        scale = rdeg[here, :]
        dsc[rows_at(512 + start, 512), :] = (back * jnp.concatenate([scale, scale], axis=1)).astype(BF)
        return carry

    hub_terms(1 - c, True)
    lax.fori_loop(0, 4, layer, 0)

    gpart[:, :, :, 32:40, :] = jnp.zeros((2, 4, 4, 8, TILE), F32)
    for which, left in ((0, feat[...].reshape(ROWS, WIDTH)), (1, agg[...])):
        part = lax.dot_general(left, dpre[...], TN, preferred_element_type=F32).reshape(4, 4, 16, WIDTH)
        gpart[which, :, :, 0:16, :] = part[..., :TILE]
        gpart[which, :, :, 16:32, :] = part[..., TILE:]
    part = jnp.dot(jnp.ones((16, ROWS), BF), dpre[...], preferred_element_type=F32)
    row8 = lax.broadcasted_iota(I32, (8, TILE), 0)
    gpart[0, 0, 0, 32:40, :] = jnp.where(row8 == 0, part[:8, :TILE], jnp.where(row8 == 1, part[:8, TILE:], 0.0))
    copy_gc = remote(gpart.at[1 - c], gcore, gc_s.at[0], gc_r.at[0], partner)
    copy_gc.start()
    pending.append(copy_gc)

    def plane(n):
        return (x + n // 4) % 4, (y + n % 4) % 4

    def g_core():
        copy_gc.wait_recv()
        total = gpart[c] + gcore[...]
        gsum[...] = total
        gsend[...] = jnp.concatenate([total, jnp.zeros((4, 4, 8, TILE), F32)], axis=2).astype(BF)

        def send(n, carry):
            px, py = plane(n)
            remote(gsend.at[py, px], gxy.at[n], gxy_s.at[n], gxy_r.at[n], device(z, px, py, c)).start()
            return carry

        lax.fori_loop(1, 16, send, 0)

    def g_plane():
        def add(n, total):
            remote(gsend.at[y, x], gxy.at[n], gxy_s.at[n], gxy_r.at[n], partner).wait_recv()
            return total + gxy[n, 0:40, :].astype(F32)

        gz[z] = lax.fori_loop(1, 16, add, gsum[y, x])
        for k in (1, 3, 2):
            copy = remote(gz.at[z], gz.at[z], gz_s.at[k - 1], gz_r.at[k - 1], device(*peer(0, k), c))
            copy.start()
            pending.append(copy)

    def g_z():
        for k in (1, 2, 3):
            slot = gz.at[(z + 4 - k) % 4]
            remote(slot, slot, gz_s.at[k - 1], gz_r.at[k - 1], partner).wait_recv()
        total = (gz[0] + gz[1] + gz[2] + gz[3]) * (1.0 / 512.0)
        gall[c, y, x] = jnp.concatenate([total, jnp.zeros((8, TILE), F32)], axis=0).astype(BF)
        piece = gall.at[c, y, x]

        def send(n, carry):
            px, py = plane(n)
            remote(piece, piece, gg_s.at[n], gg_r.at[n], device(z, px, py, c)).start()
            return carry

        lax.fori_loop(1, 16, send, 0)

    def g_gather():
        def wait(n, carry):
            slot = gall.at[c, (y + 4 - n % 4) % 4, (x + 4 - n // 4) % 4]
            remote(slot, slot, gg_s.at[n], gg_r.at[n], partner).wait_recv()
            return carry

        lax.fori_loop(1, 16, wait, 0)
        piece = gall.at[c]
        copy = remote(piece, piece, gh_s.at[0], gh_r.at[0], partner)
        copy.start()
        pending.append(copy)

    def g_done():
        slot = gall.at[1 - c]
        remote(slot, slot, gh_s.at[0], gh_r.at[0], partner).wait_recv()

    def hub_part(zc):
        left = counts[zc].reshape(1024, ROWS)
        value = jnp.dot(left, dsc[512 : 512 + ROWS, :], preferred_element_type=F32)
        hubp[zc] = value.astype(BF).reshape(4, 4, 2, 32, WIDTH)
        remote(hubp.at[zc, :, :, 1 - c], hubc.at[zc], hc_s.at[zc], hc_r.at[zc], partner).start()

    def hub_add(zc):
        remote(hubp.at[zc, :, :, 1 - c], hubc.at[zc], hc_s.at[zc], hc_r.at[zc], partner).wait_recv()
        for i in range(4):
            total = (hubp[zc, i, :, c].astype(F32) + hubc[zc, i].astype(F32)).astype(BF)
            hubs[0, zc, i] = total[..., :TILE]
            hubs[1, zc, i] = total[..., TILE:]

    def send_a(zc):
        for k in (2, 1, 3):
            for half in range(2):
                source = hubs.at[0, zc, (x + k) % 4] if half == 0 else hubs.at[1, zc, :, (y + k) % 4]
                remote(
                    source, recv_a.at[half, k - 1, zc], ha_s.at[half, k - 1, zc], ha_r.at[half, k - 1, zc],
                    device(*peer(1 + half, k), c),
                ).start()

    def collect(zc):
        for k in range(3):
            for half in range(2):
                block = recv_a.at[half, k, zc]
                remote(block, block, ha_s.at[half, k, zc], ha_r.at[half, k, zc], partner).wait_recv()
        totals = []
        for half in range(2):
            total = (hubs[0, zc, x] if half == 0 else hubs[1, zc, :, y]).astype(F32)
            for k in range(3):
                total = total + recv_a[half, k, zc].astype(F32)
            totals.append(total)
        return totals

    def send_b(k):
        for half, total in enumerate(collect((z + k) % 4)):
            out_b[k - 1, half] = total.astype(BF)
        remote(out_b.at[k - 1], recv_b.at[k - 1], hb_s.at[k - 1], hb_r.at[k - 1], device(*peer(0, k), c)).start()

    def send_c():
        for k in range(3):
            remote(recv_b.at[k], recv_b.at[k], hb_s.at[k], hb_r.at[k], partner).wait_recv()
        for half in range(2):
            total = sum_a[half]
            for k in range(3):
                total = total + recv_b[k, half].astype(F32)
            sum_b[half] = total
        for k in (2, 1, 3):
            for half, dim in ((0, 2), (1, 1)):
                copy = remote(
                    sum_b.at[half, (at[dim] + k) % 4], recv_c.at[half, k - 1],
                    hd_s.at[half, k - 1], hd_r.at[half, k - 1], device(*peer(dim, k), c),
                )
                copy.start()
                pending.append(copy)

    def hub_total(half):
        for k in range(3):
            remote(recv_c.at[half, k], recv_c.at[half, k], hd_s.at[half, k], hd_r.at[half, k], partner).wait_recv()
        return sum_b[half, at[2 - half]] + recv_c[half, 0] + recv_c[half, 1] + recv_c[half, 2]

    def merge(r, carry):
        weight = [[(tcol[k, r] == r + o).astype(F32) for k in range(SLOTS)] for o in range(5)]
        for s in range(4):
            part = pl.ds(s * 32, 32)
            total = [jnp.zeros((32, TILE), F32) for _ in range(5)]
            for k in range(SLOTS):
                value = bits[r, k, part, :].astype(F32)
                for o in range(5):
                    total[o] = total[o] + value * weight[o][k]
            for o in range(5):
                merged[r + 4, o, part, :] = total[o].astype(BF)
        return carry

    def order(i):
        return jnp.where(i == 0, 2, jnp.where(i == 1, 1, jnp.where(i == 2, 3, 0)))

    merged[0:4] = jnp.zeros((4, 5, TILE, TILE), BF)
    merged[20:24] = jnp.zeros((4, 5, TILE, TILE), BF)

    def step(i, carry):
        @pl.when(i < 4)
        def _():
            hub_part((z + order(i)) % 4)

        @pl.when(i == 1)
        def _():
            g_core()

        @pl.when(i >= 4)
        def _():
            lax.fori_loop((i - 4) * 4, (i - 3) * 4, merge, 0)

        @pl.when(i >= 2)
        def _():
            zc = (z + order(i - 2)) % 4
            hub_add(zc)
            send_a(zc)

        return carry

    lax.fori_loop(0, 6, step, 0)
    g_plane()

    def step_b(i, carry):
        lax.fori_loop(8 + i * 2, 10 + i * 2, merge, 0)
        send_b(order(i))
        return carry

    lax.fori_loop(0, 3, step_b, 0)
    g_z()
    lax.fori_loop(14, 16, merge, 0)
    for half, total in enumerate(collect(z)):
        sum_a[half] = total

    dsc[0:512, :] = jnp.zeros((512, WIDTH), BF)
    dsc[512 + ROWS :, :] = jnp.zeros((512, WIDTH), BF)

    def transposed(t):
        left = jnp.concatenate([merged[t + q, 4 - q] for q in range(5)], axis=0)
        right = dsc[pl.ds(pl.multiple_of(t * TILE, TILE), 5 * TILE), :]
        return lax.dot_general(left, right, TN, preferred_element_type=F32)

    for side, start in ((0, 0), (1, 18)):
        for i in range(2):
            rim_out[side, i * TILE : (i + 1) * TILE, :] = transposed(start + i).astype(BF)
    rim_low = remote(rim_out.at[0], rim_in.at[0], rim_s.at[0], rim_r.at[0], before)
    rim_high = remote(rim_out.at[1], rim_in.at[1], rim_s.at[1], rim_r.at[1], after)
    rim_low.start()
    rim_high.start()
    pending.extend((rim_low, rim_high))

    def interior(t, carry):
        here = rows_at(t * TILE, TILE)
        value = transposed(t + 2)
        value = value + lax.dot_general(dpre[here, :], ws[...], NT, preferred_element_type=F32)
        base[here, :] = value
        return carry

    lax.fori_loop(0, 4, interior, 0)
    send_c()
    lax.fori_loop(4, 16, interior, 0)
    g_gather()
    rim_low.wait_recv()
    rim_high.wait_recv()
    low = jnp.where(me == 0, 0.0, rim_in[1].astype(F32))
    base[:HALO, :] = base[:HALO, :] + low
    high = jnp.where(me == 127, 0.0, rim_in[0].astype(F32))
    base[ROWS - HALO :, :] = base[ROWS - HALO :, :] + high
    for copy in pending[:early]:
        copy.wait_send()

    def sent_parts(zc, carry):
        remote(hubc.at[zc], hubc.at[zc], hc_s.at[zc], hc_r.at[zc], partner).wait_send()
        for k in range(3):
            for half in range(2):
                block = recv_a.at[half, k, zc]
                remote(block, block, ha_s.at[half, k, zc], ha_r.at[half, k, zc], partner).wait_send()
        return carry

    def sent_plane(n, carry):
        remote(gsend.at[y, x], gxy.at[n], gxy_s.at[n], gxy_r.at[n], partner).wait_send()
        return carry

    lax.fori_loop(0, 4, sent_parts, 0)
    lax.fori_loop(1, 16, sent_plane, 0)
    for k in range(3):
        remote(recv_b.at[k], recv_b.at[k], hb_s.at[k], hb_r.at[k], partner).wait_send()
    total = jnp.concatenate([hub_total(0), hub_total(1)], axis=1)
    upper = total.astype(BF)
    lower = (total - upper.astype(F32)).astype(BF)
    right = jnp.concatenate([upper, lower, jnp.zeros((64, WIDTH), BF)], axis=0)

    def finish(j, carry):
        here = rows_at(j * 256, 256)
        ids = lax.broadcasted_iota(I32, (256, TILE), 0) + j * 256
        place = (ids == hub_row).astype(F32).astype(BF)
        value = base[here, :] + jnp.dot(place, right, preferred_element_type=F32)
        fgrad[here, :] = value.astype(BF)
        return carry

    lax.fori_loop(0, 8, finish, 0)
    g_done()
    sums[...] = gall[...]
    for copy in pending[early:]:
        copy.wait_send()

    def sent_gather(n, carry):
        remote(gall.at[c, y, x], gall.at[c, y, x], gg_s.at[n], gg_r.at[n], partner).wait_send()
        return carry

    lax.fori_loop(1, 16, sent_gather, 0)


def deliver(hid, fgrad, gall, hidden_out, grad_out, self_out, neighbor_out, bias_out, sem):
    copies = []
    for i, (source, target) in enumerate(((hid, hidden_out), (fgrad, grad_out))):
        for q in range(4):
            rows = pl.ds(q * 512, 512)
            copies.append(pltpu.make_async_copy(source.at[rows], target.at[rows], sem.at[i * 4 + q]))
    for copy in copies:
        copy.start()
    for which, out in ((0, self_out), (1, neighbor_out)):
        out[:, :TILE] = gall[which, :, :, 0:16, :].astype(F32).reshape(WIDTH, TILE)
        out[:, TILE:] = gall[which, :, :, 16:32, :].astype(F32).reshape(WIDTH, TILE)
    bias_row = gall[0, 0, 0, 32:40, :].astype(F32)
    bias_out[:, :TILE] = bias_row[0:1, :]
    bias_out[:, TILE:] = bias_row[1:2, :]
    for copy in copies:
        copy.wait()


SCRATCH = [
    VMEM((TILES, TILE, WIDTH), BF),
    VMEM((6, TILE, WIDTH), BF),
    VMEM((6, TILE, WIDTH), BF),
    VMEM((TILES, SLOTS, TILE, TILE), I32),
    VMEM((ROWS, WIDTH), BF),
    VMEM((WIDTH, WIDTH), BF),
    VMEM((WIDTH, WIDTH), BF),
    VMEM((1, WIDTH), F32),
    VMEM((4, ROWS), I32),
    VMEM((4, ROWS), I32),
    VMEM((TILES, TILE), I32),
    VMEM((2, 4, 4, 4, 2, 32, TILE), BF),
    VMEM((4, 16, 2, 32, ROWS), BF),
    VMEM((4, ROWS), I32),
    VMEM((4, ROWS), I32),
    VMEM((4, 256, 512), BF),
    VMEM((24, 5, TILE, TILE), BF),
    VMEM((ROWS, WIDTH), F32),
    VMEM((ROWS, WIDTH), F32),
    VMEM((ROWS, TILE), F32),
    VMEM((ROWS, WIDTH), BF),
    VMEM((ROWS, WIDTH), BF),
    VMEM((ROWS + 1024, WIDTH), BF),
    VMEM((ROWS, WIDTH), F32),
    VMEM((2, HALO, WIDTH), BF),
    VMEM((2, HALO, WIDTH), BF),
    VMEM((4, 4, 4, 2, 32, WIDTH), BF),
    VMEM((4, 4, 4, 32, WIDTH), BF),
    VMEM((2, 4, 4, 4, 32, TILE), BF),
    VMEM((2, 3, 4, 4, 32, TILE), BF),
    VMEM((2, 4, 32, TILE), F32),
    VMEM((3, 2, 4, 32, TILE), BF),
    VMEM((3, 2, 4, 32, TILE), BF),
    VMEM((2, 4, 32, TILE), F32),
    VMEM((2, 3, 32, TILE), F32),
    VMEM((2, 4, 4, 40, TILE), F32),
    VMEM((4, 4, 40, TILE), F32),
    VMEM((4, 4, 40, TILE), F32),
    VMEM((4, 4, 48, TILE), BF),
    VMEM((16, 48, TILE), BF),
    VMEM((4, 40, TILE), F32),
    VMEM((2, 4, 4, 48, TILE), BF),
    DMA((8,)), DMA((4,)), DMA((TILES,)),
    DMA((2,)), DMA((2,)),
    DMA((2, 2, 3)), DMA((2, 2, 3)),
    DMA((2, 4, 3)), DMA((2, 4, 3)),
    DMA((8,)), DMA((8,)),
    DMA((2,)), DMA((2,)),
    DMA((4,)), DMA((4,)),
    DMA((2, 3, 4)), DMA((2, 3, 4)), DMA((3,)), DMA((3,)), DMA((2, 3)), DMA((2, 3)),
    DMA((1,)), DMA((1,)),
    DMA((16,)), DMA((16,)),
    DMA((3,)), DMA((3,)),
    DMA((16,)), DMA((16,)),
    DMA((1,)), DMA((1,)),
]


def local(
    features, self_weight, neighbor_weight, bias_term, tile_columns, tile_bits,
    hub_slots, hub_live, degree, hub_rows, cotangent,
):
    smem = pl.BlockSpec(memory_space=pltpu.SMEM)
    vmem = pl.BlockSpec(memory_space=VMEM)
    hbm = pl.BlockSpec(memory_space=pl.ANY)
    wide = jax.ShapeDtypeStruct((ROWS, WIDTH), BF)
    hidden, feature_grad, sums = pl.pallas_call(
        kernel,
        out_shape=(VMEM(wide.shape, BF), VMEM(wide.shape, BF), VMEM((2, 4, 4, 48, TILE), BF)),
        in_specs=[smem, smem] + [hbm] * 9,
        out_specs=(vmem, vmem, vmem),
        scratch_shapes=SCRATCH,
        name="sage_layer",
        compiler_params=pltpu.CompilerParams(
            collective_id=0, has_side_effects=True, vmem_limit_bytes=56 * 2**20
        ),
    )(
        tile_columns.T, hub_rows, features.reshape(TILES, TILE, WIDTH), tile_bits, cotangent, self_weight, neighbor_weight,
        bias_term.reshape(1, WIDTH), hub_slots.T, hub_live.T, degree.reshape(TILES, TILE),
    )
    square = jax.ShapeDtypeStruct((WIDTH, WIDTH), F32)
    hidden, feature_grad, self_grad, neighbor_grad, bias_grad = pl.pallas_call(
        deliver,
        out_shape=(wide, wide, square, square, jax.ShapeDtypeStruct((1, WIDTH), F32)),
        in_specs=[vmem, vmem, vmem],
        out_specs=(hbm, hbm, vmem, vmem, vmem),
        scratch_shapes=[DMA((8,))],
        compiler_params=pltpu.CompilerParams(vmem_limit_bytes=8 * 2**20),
        name="deliver",
    )(*(pltpu.with_memory_space_constraint(value, VMEM) for value in (hidden, feature_grad, sums)))
    return hidden, feature_grad, self_grad, neighbor_grad, bias_grad.reshape(WIDTH)


def solution(mesh):
    placed = (
        P("band", None), P(), P(), P(), P("band", None), P("band", None, None, None),
        P("band", None), P("band", None), P("band"), P("band"), P("band", None),
    )
    return jax.shard_map(
        local,
        mesh=mesh,
        in_specs=placed,
        out_specs=(P("band", None), P("band", None), P(), P(), P()),
        check_vma=False,
    )
```

```python
import math

import jax
import jax.numpy as jnp
from jax import lax
from jax.experimental import pallas as pl
from jax.experimental.pallas import tpu as pltpu
from jax.sharding import PartitionSpec as P

MESH = pl.DeviceIdType.MESH
BF = jnp.bfloat16
F32 = jnp.float32
I32 = jnp.int32
VMEM = pltpu.VMEM
DMA = pltpu.SemaphoreType.DMA

ROWS = 2048
WIDTH = 256
TILE = 128
TILES = 16
SLOTS = 6
HALO = 256
HUBS = 4096
ORDERS = ((0, 1, 2), (1, 2, 0))
PLANE = [(i, j) for i in range(4) for j in range(4) if (i, j) != (0, 0)]
TN = (((0,), (0,)), ((), ()))
NT = (((1,), (1,)), ((), ()))


def device(z, x, y, c):
    return ((z * 4 + x) * 4 + y) * 2 + c


def rows_at(start, size):
    return pl.ds(pl.multiple_of(start, size), size)


def remote(src, dst, send, recv, target):
    return pltpu.make_async_remote_copy(
        src_ref=src, dst_ref=dst, send_sem=send, recv_sem=recv, device_id=(target,), device_id_type=MESH
    )


def kernel(
    tcol, hrow, feat_hbm, bits_hbm, cot_hbm, ws_hbm, wn_hbm, bias_hbm, slots_hbm, live_hbm, deg_hbm,
    hid, fgrad, sums,
    feat, low, high, bits, cot, ws, wn, bias, slots, live, deg, table, counts, slot_low, slot_high, onehot, merged, band, pre0,
    rdeg, agg, dpre, dsc, base, rim_out, rim_in,
    hubp, hubc, hubs, recv_a, sum_a, out_b, recv_b, sum_b, recv_c,
    gpart, gcore, gsum, gsend, gxy, gz, gall,
    load_sem, feat_sem, bits_sem, halo_s, halo_r, ag_s, ag_r, line_s, line_r, core_s, core_r, rim_s, rim_r,
    hc_s, hc_r, ha_s, ha_r, hb_s, hb_r, hd_s, hd_r,
    gc_s, gc_r, gxy_s, gxy_r, gz_s, gz_r, gg_s, gg_r, gh_s, gh_r,
):
    me = lax.axis_index("band")
    z, x, y, c = me // 32, (me // 8) % 4, (me // 2) % 4, me % 2
    at = (z, x, y)
    partner = device(z, x, y, 1 - c)
    after, before = (me + 1) % 128, (me + 127) % 128

    def peer(dim, k):
        place = list(at)
        place[dim] = (place[dim] + k) % 4
        return tuple(place)

    load_f = [
        pltpu.make_async_copy(feat_hbm.at[q * 4 : q * 4 + 4], feat.at[q * 4 : q * 4 + 4], feat_sem.at[q]) for q in range(4)
    ]
    for load in load_f:
        load.start()
    small = [
        pltpu.make_async_copy(source, target, load_sem.at[2 + i])
        for i, (source, target) in enumerate(
            ((slots_hbm, slots), (live_hbm, live), (ws_hbm, ws), (wn_hbm, wn), (bias_hbm, bias), (deg_hbm, deg))
        )
    ]
    barrier = pltpu.get_barrier_semaphore()
    greeted = [partner, after, before]
    greeted.extend(device(*peer(0, k), c) for k in (1, 2, 3))
    greeted.extend(device(z, (x + i) % 4, (y + j) % 4, c) for i, j in PLANE)
    for other in greeted:
        pl.semaphore_signal(barrier, inc=1, device_id=(other,), device_id_type=MESH)
    for load in small:
        load.start()
    load_c = pltpu.make_async_copy(cot_hbm, cot, load_sem.at[1])
    bit_loads = []
    for r in range(TILES):
        load = pltpu.make_async_copy(bits_hbm.at[r], bits.at[r], bits_sem.at[r])
        bit_loads.append(load)

    lane = lax.broadcasted_iota(I32, (32, TILE), 1)
    sub = lax.broadcasted_iota(I32, (32, TILE), 0)
    hub_col = jnp.full((32, TILE), -1, I32)
    hub_row = jnp.full((1, TILE), -1, I32)
    lane1 = lax.broadcasted_iota(I32, (1, TILE), 1)
    for h in range(32):
        value = hrow[h]
        hub_col = jnp.where(sub == h, value, hub_col)
        hub_row = jnp.where((lane1 == h) | (lane1 == h + 32), value, hub_row)
    pick = jnp.concatenate(
        [(hub_col == lane + j * TILE).astype(F32).astype(BF) for j in range(TILES)], axis=1
    )
    own = jnp.zeros((32, WIDTH), F32)
    for q in range(4):
        load_f[q].wait()
        rows = feat[q * 4 : q * 4 + 4].reshape(512, WIDTH)
        own = own + jnp.dot(pick[:, q * 512 : q * 512 + 512], rows, preferred_element_type=F32)
    own = own.astype(BF)
    table[0, z, x, y, c] = own[:, :TILE]
    table[1, z, x, y, c] = own[:, TILE:]

    pl.semaphore_wait(barrier, len(greeted))

    def line(half, place, core, free):
        index = [half] + [slice(None) if d in free else place[d] for d in range(3)] + [core]
        return table.at[tuple(index)]

    pending = []

    def gather_send(phase, half):
        dim, free = ORDERS[half][phase], ORDERS[half][:phase]
        block = line(half, at, c, free)
        for k in (1, 3, 2):
            copy = remote(block, block, ag_s.at[phase, half, k - 1], ag_r.at[phase, half, k - 1], device(*peer(dim, k), c))
            copy.start()
            pending.append(copy)

    def gather_recv(phase, half, k):
        dim, free = ORDERS[half][phase], ORDERS[half][:phase]
        block = line(half, peer(dim, 4 - k), c, free)
        remote(block, block, ag_s.at[phase, half, k - 1], ag_r.at[phase, half, k - 1], device(*peer(dim, k), c)).wait_recv()

    def line_send(half, k):
        middle, last = ORDERS[half][1:]
        block = line(half, peer(middle, (4 - k) % 4), c, ORDERS[half][:1])
        for i in (1, 3, 2):
            copy = remote(block, block, line_s.at[half, k, i - 1], line_r.at[half, k, i - 1], device(*peer(last, i), c))
            copy.start()
            pending.append(copy)

    def line_recv(half, i):
        middle, last = ORDERS[half][1:]
        place = list(peer(last, 4 - i))
        for k in range(4):
            piece = list(place)
            piece[middle] = (piece[middle] + 4 - k) % 4
            block = line(half, piece, c, ORDERS[half][:1])
            remote(block, block, line_s.at[half, k, i - 1], line_r.at[half, k, i - 1], partner).wait_recv()
        return line(half, place, c, ORDERS[half][:2])

    def core_send(block, n):
        copy = remote(block, block, core_s.at[n], core_r.at[n], partner)
        copy.start()
        pending.append(copy)

    def core_recv(half, place, n):
        block = line(half, place, 1 - c, ORDERS[half][:2])
        remote(block, block, core_s.at[n], core_r.at[n], partner).wait_recv()

    gather_send(0, 0)
    gather_send(0, 1)
    for load in bit_loads:
        load.start()
    load_c.start()

    for load in small:
        load.wait()
    named = jnp.where(live[...] == 1, slots[...], -1)
    slot_low[...] = named & 255
    slot_high[...] = named >> 8
    span = 512

    def build(j, carry):
        cols = rows_at(j * span, span)
        ids = lax.broadcasted_iota(I32, (256, span), 0).astype(jnp.int16)
        for k in range(4):
            value = jnp.broadcast_to(slot_low[k : k + 1, cols], (16, span)).astype(jnp.int16)
            value = jnp.broadcast_to(value[None], (16, 16, span)).reshape(256, span)
            onehot[k] = jnp.where(value == ids, jnp.ones((), BF), jnp.zeros((), BF))

        def block(h, carry):
            total = jnp.zeros((256, span), BF)
            for k in range(4):
                keep = jnp.broadcast_to(jnp.where(slot_high[k : k + 1, cols] == h, 1.0, 0.0), (16, span)).astype(BF)
                keep = jnp.broadcast_to(keep[None], (16, 16, span)).reshape(256, span)
                total = total + onehot[k] * keep
            counts[h // 4, pl.ds((h % 4) * 4, 4), :, :, cols] = total.reshape(4, 2, 32, span)
            return carry

        return lax.fori_loop(0, HUBS // 256, block, carry)

    lax.fori_loop(0, 2, build, 0)
    for half in range(2):
        for k in (1, 3, 2):
            gather_recv(0, half, k)
        gather_send(1, half)
        line_send(half, 0)
    lax.fori_loop(2, 4, build, 0)
    for k in (1, 3, 2):
        for half in range(2):
            gather_recv(1, half, k)
            line_send(half, k)
    halo_low = remote(feat.at[0:2], high.at[4:6], halo_s.at[0], halo_r.at[0], before)
    halo_high = remote(feat.at[14:16], low.at[0:2], halo_s.at[1], halo_r.at[1], after)
    halo_low.start()
    halo_high.start()
    pending.extend((halo_low, halo_high))
    for half in range(2):
        core_send(line(half, at, c, ORDERS[half][:2]), half)

    def own_term(j, carry):
        here = rows_at(j * 256, 256)
        pre0[here, :] = jnp.dot(feat[pl.ds(j * 2, 2)].reshape(256, WIDTH), ws[...], preferred_element_type=F32) + bias[...]
        return carry

    def divide(r, carry):
        row = 1.0 / deg[pl.ds(r, 1), :].astype(F32)
        rdeg[rows_at(r * TILE, TILE), :] = jnp.broadcast_to(row, (TILE, TILE)).T
        return carry

    def forward(rows, first):
        def body(r, carry):
            pltpu.make_async_copy(bits_hbm.at[r], bits.at[r], bits_sem.at[r]).wait()
            left = jnp.concatenate([bits[r, k].astype(F32).astype(BF) for k in range(SLOTS)], axis=1)
            right = jnp.concatenate([rows[jnp.clip(tcol[k, r] - first, 0, rows.shape[0] - 1)] for k in range(SLOTS)], axis=0)
            band[rows_at(r * TILE, TILE), :] = jnp.dot(left, right, preferred_element_type=F32)
            return carry

        return body

    lax.fori_loop(0, 8, own_term, 0)
    lax.fori_loop(0, TILES, divide, 0)
    lax.fori_loop(2, 8, forward(feat, 2), 0)
    n = 2
    for k in (1, 3):
        for half in range(2):
            core_send(line_recv(half, k), n)
            n += 1
    lax.fori_loop(8, 14, forward(feat, 2), 0)
    for half in range(2):
        core_send(line_recv(half, 2), n)
        n += 1

    def hub_terms(core, add):
        def nodes(j, carry):
            cols = rows_at(j * 1024, 1024)
            right = jnp.concatenate([table[half, :, :, :, core].reshape(HUBS // 2, TILE) for half in range(2)], axis=1)
            left = counts[:, :, core, :, cols].reshape(HUBS // 2, 1024)
            value = lax.dot_general(left, right, TN, preferred_element_type=F32)
            base[cols, :] = base[cols, :] + value if add else value
            return carry

        lax.fori_loop(0, 2, nodes, 0)

    hub_terms(c, False)
    low[2:6] = feat[0:4]
    high[0:4] = feat[12:16]
    halo_low.wait_recv()
    halo_high.wait_recv()
    low[0:2] = jnp.where(me == 0, 0.0, low[0:2].astype(F32)).astype(BF)
    high[4:6] = jnp.where(me == 127, 0.0, high[4:6].astype(F32)).astype(BF)
    lax.fori_loop(0, 2, forward(low, 0), 0)
    lax.fori_loop(14, 16, forward(high, 14), 0)

    n = 0
    for k in (0, 1, 3, 2):
        for half in range(2):
            core_recv(half, peer(ORDERS[half][2], (4 - k) % 4), n)
            n += 1

    early = len(pending)

    load_c.wait()

    def layer(i, carry):
        start = i * 512
        here = rows_at(start, 512)
        for s in range(8):
            part = rows_at(start + s * 64, 64)
            scale = rdeg[part, :]
            total = band[part, :] + base[part, :]
            agg[part, :] = (total * jnp.concatenate([scale, scale], axis=1)).astype(BF)
        pre = pre0[here, :] + jnp.dot(agg[here, :], wn[...], preferred_element_type=F32)
        for s in range(8):
            part = rows_at(start + s * 64, 64)
            v = pre[s * 64 : s * 64 + 64, :]
            sig = 0.5 * jnp.tanh(0.5 * v) + 0.5
            act = v * sig
            hid[part, :] = act.astype(BF)
            dpre[part, :] = (cot[part, :].astype(F32) * sig * (1.0 + v - act)).astype(BF)
        back = lax.dot_general(dpre[here, :], wn[...], NT, preferred_element_type=F32)
        scale = rdeg[here, :]
        dsc[rows_at(512 + start, 512), :] = (back * jnp.concatenate([scale, scale], axis=1)).astype(BF)
        return carry

    hub_terms(1 - c, True)
    lax.fori_loop(0, 4, layer, 0)

    gpart[:, :, :, 32:40, :] = jnp.zeros((2, 4, 4, 8, TILE), F32)
    for which, left in ((0, feat[...].reshape(ROWS, WIDTH)), (1, agg[...])):
        part = lax.dot_general(left, dpre[...], TN, preferred_element_type=F32).reshape(4, 4, 16, WIDTH)
        gpart[which, :, :, 0:16, :] = part[..., :TILE]
        gpart[which, :, :, 16:32, :] = part[..., TILE:]
    part = jnp.dot(jnp.ones((16, ROWS), BF), dpre[...], preferred_element_type=F32)
    row8 = lax.broadcasted_iota(I32, (8, TILE), 0)
    gpart[0, 0, 0, 32:40, :] = jnp.where(row8 == 0, part[:8, :TILE], jnp.where(row8 == 1, part[:8, TILE:], 0.0))
    copy_gc = remote(gpart.at[1 - c], gcore, gc_s.at[0], gc_r.at[0], partner)
    copy_gc.start()
    pending.append(copy_gc)

    def plane(n):
        return (x + n // 4) % 4, (y + n % 4) % 4

    def g_core():
        copy_gc.wait_recv()
        total = gpart[c] + gcore[...]
        gsum[...] = total
        gsend[...] = jnp.concatenate([total, jnp.zeros((4, 4, 8, TILE), F32)], axis=2).astype(BF)

        def send(n, carry):
            px, py = plane(n)
            remote(gsend.at[py, px], gxy.at[n], gxy_s.at[n], gxy_r.at[n], device(z, px, py, c)).start()
            return carry

        lax.fori_loop(1, 16, send, 0)

    def g_plane():
        def add(n, total):
            remote(gsend.at[y, x], gxy.at[n], gxy_s.at[n], gxy_r.at[n], partner).wait_recv()
            return total + gxy[n, 0:40, :].astype(F32)

        gz[z] = lax.fori_loop(1, 16, add, gsum[y, x])
        for k in (1, 3, 2):
            copy = remote(gz.at[z], gz.at[z], gz_s.at[k - 1], gz_r.at[k - 1], device(*peer(0, k), c))
            copy.start()
            pending.append(copy)

    def g_z():
        for k in (1, 2, 3):
            slot = gz.at[(z + 4 - k) % 4]
            remote(slot, slot, gz_s.at[k - 1], gz_r.at[k - 1], partner).wait_recv()
        total = (gz[0] + gz[1] + gz[2] + gz[3]) * (1.0 / 512.0)
        gall[c, y, x] = jnp.concatenate([total, jnp.zeros((8, TILE), F32)], axis=0).astype(BF)
        piece = gall.at[c, y, x]

        def send(n, carry):
            px, py = plane(n)
            remote(piece, piece, gg_s.at[n], gg_r.at[n], device(z, px, py, c)).start()
            return carry

        lax.fori_loop(1, 16, send, 0)

    def g_gather():
        def wait(n, carry):
            slot = gall.at[c, (y + 4 - n % 4) % 4, (x + 4 - n // 4) % 4]
            remote(slot, slot, gg_s.at[n], gg_r.at[n], partner).wait_recv()
            return carry

        lax.fori_loop(1, 16, wait, 0)
        piece = gall.at[c]
        copy = remote(piece, piece, gh_s.at[0], gh_r.at[0], partner)
        copy.start()
        pending.append(copy)

    def g_done():
        slot = gall.at[1 - c]
        remote(slot, slot, gh_s.at[0], gh_r.at[0], partner).wait_recv()

    def hub_part(zc):
        left = counts[zc].reshape(1024, ROWS)
        value = jnp.dot(left, dsc[512 : 512 + ROWS, :], preferred_element_type=F32)
        hubp[zc] = value.astype(BF).reshape(4, 4, 2, 32, WIDTH)
        remote(hubp.at[zc, :, :, 1 - c], hubc.at[zc], hc_s.at[zc], hc_r.at[zc], partner).start()

    def hub_add(zc):
        remote(hubp.at[zc, :, :, 1 - c], hubc.at[zc], hc_s.at[zc], hc_r.at[zc], partner).wait_recv()
        for i in range(4):
            total = (hubp[zc, i, :, c].astype(F32) + hubc[zc, i].astype(F32)).astype(BF)
            hubs[0, zc, i] = total[..., :TILE]
            hubs[1, zc, i] = total[..., TILE:]

    def send_a(zc):
        for k in (2, 1, 3):
            for half in range(2):
                source = hubs.at[0, zc, (x + k) % 4] if half == 0 else hubs.at[1, zc, :, (y + k) % 4]
                remote(
                    source, recv_a.at[half, k - 1, zc], ha_s.at[half, k - 1, zc], ha_r.at[half, k - 1, zc],
                    device(*peer(1 + half, k), c),
                ).start()

    def collect(zc):
        for k in range(3):
            for half in range(2):
                block = recv_a.at[half, k, zc]
                remote(block, block, ha_s.at[half, k, zc], ha_r.at[half, k, zc], partner).wait_recv()
        totals = []
        for half in range(2):
            total = (hubs[0, zc, x] if half == 0 else hubs[1, zc, :, y]).astype(F32)
            for k in range(3):
                total = total + recv_a[half, k, zc].astype(F32)
            totals.append(total)
        return totals

    def send_b(k):
        for half, total in enumerate(collect((z + k) % 4)):
            out_b[k - 1, half] = total.astype(BF)
        remote(out_b.at[k - 1], recv_b.at[k - 1], hb_s.at[k - 1], hb_r.at[k - 1], device(*peer(0, k), c)).start()

    def send_c():
        for k in range(3):
            remote(recv_b.at[k], recv_b.at[k], hb_s.at[k], hb_r.at[k], partner).wait_recv()
        for half in range(2):
            total = sum_a[half]
            for k in range(3):
                total = total + recv_b[k, half].astype(F32)
            sum_b[half] = total
        for k in (2, 1, 3):
            for half, dim in ((0, 2), (1, 1)):
                copy = remote(
                    sum_b.at[half, (at[dim] + k) % 4], recv_c.at[half, k - 1],
                    hd_s.at[half, k - 1], hd_r.at[half, k - 1], device(*peer(dim, k), c),
                )
                copy.start()
                pending.append(copy)

    def hub_total(half):
        for k in range(3):
            remote(recv_c.at[half, k], recv_c.at[half, k], hd_s.at[half, k], hd_r.at[half, k], partner).wait_recv()
        return sum_b[half, at[2 - half]] + recv_c[half, 0] + recv_c[half, 1] + recv_c[half, 2]

    def merge(r, carry):
        weight = [[(tcol[k, r] == r + o).astype(F32) for k in range(SLOTS)] for o in range(5)]
        for s in range(4):
            part = pl.ds(s * 32, 32)
            total = [jnp.zeros((32, TILE), F32) for _ in range(5)]
            for k in range(SLOTS):
                value = bits[r, k, part, :].astype(F32)
                for o in range(5):
                    total[o] = total[o] + value * weight[o][k]
            for o in range(5):
                merged[r + 4, o, part, :] = total[o].astype(BF)
        return carry

    def order(i):
        return jnp.where(i == 0, 2, jnp.where(i == 1, 1, jnp.where(i == 2, 3, 0)))

    merged[0:4] = jnp.zeros((4, 5, TILE, TILE), BF)
    merged[20:24] = jnp.zeros((4, 5, TILE, TILE), BF)

    def step(i, carry):
        @pl.when(i < 4)
        def _():
            hub_part((z + order(i)) % 4)

        @pl.when(i == 1)
        def _():
            g_core()

        @pl.when(i >= 4)
        def _():
            lax.fori_loop((i - 4) * 4, (i - 3) * 4, merge, 0)

        @pl.when(i >= 2)
        def _():
            zc = (z + order(i - 2)) % 4
            hub_add(zc)
            send_a(zc)

        return carry

    lax.fori_loop(0, 6, step, 0)
    g_plane()

    def step_b(i, carry):
        lax.fori_loop(8 + i * 2, 10 + i * 2, merge, 0)
        send_b(order(i))
        return carry

    lax.fori_loop(0, 3, step_b, 0)
    g_z()
    lax.fori_loop(14, 16, merge, 0)
    for half, total in enumerate(collect(z)):
        sum_a[half] = total

    dsc[0:512, :] = jnp.zeros((512, WIDTH), BF)
    dsc[512 + ROWS :, :] = jnp.zeros((512, WIDTH), BF)

    def transposed(t):
        left = jnp.concatenate([merged[t + q, 4 - q] for q in range(5)], axis=0)
        right = dsc[pl.ds(pl.multiple_of(t * TILE, TILE), 5 * TILE), :]
        return lax.dot_general(left, right, TN, preferred_element_type=F32)

    for side, start in ((0, 0), (1, 18)):
        for i in range(2):
            rim_out[side, i * TILE : (i + 1) * TILE, :] = transposed(start + i).astype(BF)
    rim_low = remote(rim_out.at[0], rim_in.at[0], rim_s.at[0], rim_r.at[0], before)
    rim_high = remote(rim_out.at[1], rim_in.at[1], rim_s.at[1], rim_r.at[1], after)
    rim_low.start()
    rim_high.start()
    pending.extend((rim_low, rim_high))

    def interior(t, carry):
        here = rows_at(t * TILE, TILE)
        value = transposed(t + 2)
        value = value + lax.dot_general(dpre[here, :], ws[...], NT, preferred_element_type=F32)
        base[here, :] = value
        return carry

    lax.fori_loop(0, 4, interior, 0)
    send_c()
    lax.fori_loop(4, 16, interior, 0)
    g_gather()
    rim_low.wait_recv()
    rim_high.wait_recv()
    low = jnp.where(me == 0, 0.0, rim_in[1].astype(F32))
    base[:HALO, :] = base[:HALO, :] + low
    high = jnp.where(me == 127, 0.0, rim_in[0].astype(F32))
    base[ROWS - HALO :, :] = base[ROWS - HALO :, :] + high
    for copy in pending[:early]:
        copy.wait_send()

    def sent_parts(zc, carry):
        remote(hubc.at[zc], hubc.at[zc], hc_s.at[zc], hc_r.at[zc], partner).wait_send()
        for k in range(3):
            for half in range(2):
                block = recv_a.at[half, k, zc]
                remote(block, block, ha_s.at[half, k, zc], ha_r.at[half, k, zc], partner).wait_send()
        return carry

    def sent_plane(n, carry):
        remote(gsend.at[y, x], gxy.at[n], gxy_s.at[n], gxy_r.at[n], partner).wait_send()
        return carry

    lax.fori_loop(0, 4, sent_parts, 0)
    lax.fori_loop(1, 16, sent_plane, 0)
    for k in range(3):
        remote(recv_b.at[k], recv_b.at[k], hb_s.at[k], hb_r.at[k], partner).wait_send()
    total = jnp.concatenate([hub_total(0), hub_total(1)], axis=1)
    upper = total.astype(BF)
    lower = (total - upper.astype(F32)).astype(BF)
    right = jnp.concatenate([upper, lower, jnp.zeros((64, WIDTH), BF)], axis=0)

    def finish(j, carry):
        here = rows_at(j * 256, 256)
        ids = lax.broadcasted_iota(I32, (256, TILE), 0) + j * 256
        place = (ids == hub_row).astype(F32).astype(BF)
        value = base[here, :] + jnp.dot(place, right, preferred_element_type=F32)
        fgrad[here, :] = value.astype(BF)
        return carry

    lax.fori_loop(0, 8, finish, 0)
    g_done()
    sums[...] = gall[...]
    for copy in pending[early:]:
        copy.wait_send()

    def sent_gather(n, carry):
        remote(gall.at[c, y, x], gall.at[c, y, x], gg_s.at[n], gg_r.at[n], partner).wait_send()
        return carry

    lax.fori_loop(1, 16, sent_gather, 0)


def deliver(hid, fgrad, gall, hidden_out, grad_out, self_out, neighbor_out, bias_out, square, row, sem):
    copies = []
    for i, (source, target) in enumerate(((hid, hidden_out), (fgrad, grad_out))):
        for q in range(4):
            rows = pl.ds(q * 512, 512)
            copies.append(pltpu.make_async_copy(source.at[rows], target.at[rows], sem.at[i * 4 + q]))
    for copy in copies:
        copy.start()
    for which, out in ((0, self_out), (1, neighbor_out)):
        square[which, :, :TILE] = gall[which, :, :, 0:16, :].astype(F32).reshape(WIDTH, TILE)
        square[which, :, TILE:] = gall[which, :, :, 16:32, :].astype(F32).reshape(WIDTH, TILE)
        copy = pltpu.make_async_copy(square.at[which], out, sem.at[8 + which])
        copy.start()
        copies.append(copy)
    bias_row = gall[0, 0, 0, 32:40, :].astype(F32)
    row[:, :TILE] = bias_row[0:1, :]
    row[:, TILE:] = bias_row[1:2, :]
    copy = pltpu.make_async_copy(row, bias_out, sem.at[10])
    copy.start()
    copies.append(copy)
    for copy in copies:
        copy.wait()


SCRATCH = [
    VMEM((TILES, TILE, WIDTH), BF),
    VMEM((6, TILE, WIDTH), BF),
    VMEM((6, TILE, WIDTH), BF),
    VMEM((TILES, SLOTS, TILE, TILE), I32),
    VMEM((ROWS, WIDTH), BF),
    VMEM((WIDTH, WIDTH), BF),
    VMEM((WIDTH, WIDTH), BF),
    VMEM((1, WIDTH), F32),
    VMEM((4, ROWS), I32),
    VMEM((4, ROWS), I32),
    VMEM((TILES, TILE), I32),
    VMEM((2, 4, 4, 4, 2, 32, TILE), BF),
    VMEM((4, 16, 2, 32, ROWS), BF),
    VMEM((4, ROWS), I32),
    VMEM((4, ROWS), I32),
    VMEM((4, 256, 512), BF),
    VMEM((24, 5, TILE, TILE), BF),
    VMEM((ROWS, WIDTH), F32),
    VMEM((ROWS, WIDTH), F32),
    VMEM((ROWS, TILE), F32),
    VMEM((ROWS, WIDTH), BF),
    VMEM((ROWS, WIDTH), BF),
    VMEM((ROWS + 1024, WIDTH), BF),
    VMEM((ROWS, WIDTH), F32),
    VMEM((2, HALO, WIDTH), BF),
    VMEM((2, HALO, WIDTH), BF),
    VMEM((4, 4, 4, 2, 32, WIDTH), BF),
    VMEM((4, 4, 4, 32, WIDTH), BF),
    VMEM((2, 4, 4, 4, 32, TILE), BF),
    VMEM((2, 3, 4, 4, 32, TILE), BF),
    VMEM((2, 4, 32, TILE), F32),
    VMEM((3, 2, 4, 32, TILE), BF),
    VMEM((3, 2, 4, 32, TILE), BF),
    VMEM((2, 4, 32, TILE), F32),
    VMEM((2, 3, 32, TILE), F32),
    VMEM((2, 4, 4, 40, TILE), F32),
    VMEM((4, 4, 40, TILE), F32),
    VMEM((4, 4, 40, TILE), F32),
    VMEM((4, 4, 48, TILE), BF),
    VMEM((16, 48, TILE), BF),
    VMEM((4, 40, TILE), F32),
    VMEM((2, 4, 4, 48, TILE), BF),
    DMA((8,)), DMA((4,)), DMA((TILES,)),
    DMA((2,)), DMA((2,)),
    DMA((2, 2, 3)), DMA((2, 2, 3)),
    DMA((2, 4, 3)), DMA((2, 4, 3)),
    DMA((8,)), DMA((8,)),
    DMA((2,)), DMA((2,)),
    DMA((4,)), DMA((4,)),
    DMA((2, 3, 4)), DMA((2, 3, 4)), DMA((3,)), DMA((3,)), DMA((2, 3)), DMA((2, 3)),
    DMA((1,)), DMA((1,)),
    DMA((16,)), DMA((16,)),
    DMA((3,)), DMA((3,)),
    DMA((16,)), DMA((16,)),
    DMA((1,)), DMA((1,)),
]


def local(
    features, self_weight, neighbor_weight, bias_term, tile_columns, tile_bits,
    hub_slots, hub_live, degree, hub_rows, cotangent,
):
    smem = pl.BlockSpec(memory_space=pltpu.SMEM)
    vmem = pl.BlockSpec(memory_space=VMEM)
    hbm = pl.BlockSpec(memory_space=pl.ANY)
    wide = jax.ShapeDtypeStruct((ROWS, WIDTH), BF)
    hidden, feature_grad, sums = pl.pallas_call(
        kernel,
        out_shape=(VMEM(wide.shape, BF), VMEM(wide.shape, BF), VMEM((2, 4, 4, 48, TILE), BF)),
        in_specs=[smem, smem] + [hbm] * 9,
        out_specs=(vmem, vmem, vmem),
        scratch_shapes=SCRATCH,
        name="sage_layer",
        compiler_params=pltpu.CompilerParams(
            collective_id=0, has_side_effects=True, vmem_limit_bytes=56 * 2**20
        ),
    )(
        tile_columns.T, hub_rows, features.reshape(TILES, TILE, WIDTH), tile_bits, cotangent, self_weight, neighbor_weight,
        bias_term.reshape(1, WIDTH), hub_slots.T, hub_live.T, degree.reshape(TILES, TILE),
    )
    square = jax.ShapeDtypeStruct((WIDTH, WIDTH), F32)
    hidden, feature_grad, self_grad, neighbor_grad, bias_grad = pl.pallas_call(
        deliver,
        out_shape=(wide, wide, square, square, jax.ShapeDtypeStruct((1, WIDTH), F32)),
        in_specs=[vmem, vmem, vmem],
        out_specs=(hbm,) * 5,
        scratch_shapes=[VMEM((2, WIDTH, WIDTH), F32), VMEM((1, WIDTH), F32), DMA((11,))],
        compiler_params=pltpu.CompilerParams(vmem_limit_bytes=8 * 2**20),
        name="deliver",
    )(*(pltpu.with_memory_space_constraint(value, VMEM) for value in (hidden, feature_grad, sums)))
    return hidden, feature_grad, self_grad, neighbor_grad, bias_grad.reshape(WIDTH)


def solution(mesh):
    placed = (
        P("band", None), P(), P(), P(), P("band", None), P("band", None, None, None),
        P("band", None), P("band", None), P("band"), P("band"), P("band", None),
    )
    return jax.shard_map(
        local,
        mesh=mesh,
        in_specs=placed,
        out_specs=(P("band", None), P("band", None), P(), P(), P()),
        check_vma=False,
    )
```
